1024 devices in a mesh: dp: 16 (over z_hi, x), expert: 8 (over z_lo), tensor: 8 (over y, core).
Axes of the slice: x: 4, y: 4, z: 32 (z_hi: 4, z_lo: 8; z = z_hi * 8 + z_lo), core: 2. Of those that a mesh axis runs over, the one named last changes fastest.
Arguments:
- tokens: bfloat16 [768, 3072], P('expert', 'tensor'), may hold values from -6 to 6
- cotangent: bfloat16 [768, 3072], P('expert', 'tensor'), may hold values from -6 to 6
- expert_ids: int32 [768, 2], P('expert'), may hold values from 0 to 7, all different within a row; in each aligned block of 96 rows (0 to 95, 96 to 191, ...) at most 32 rows name the same one
- gate_probs: bfloat16 [768, 2], P('expert'), may hold values from 0.049804688 to 0.94921875
- tenant_ids: int32 [768], P('expert'), may hold values from 0 to 7
- w_gate: bfloat16 [8, 3072, 16384], P('expert', None, ('dp', 'tensor')), may hold values from -0.109375 to 0.109375
- w_up: bfloat16 [8, 3072, 16384], P('expert', None, ('dp', 'tensor')), may hold values from -0.109375 to 0.109375
- w_down: bfloat16 [8, 16384, 3072], P('expert', ('dp', 'tensor')), may hold values from -0.046875 to 0.046875
- adapter_in: bfloat16 [8, 16384, 128], P('expert', ('dp', 'tensor')), may hold values from -0.046875 to 0.046875
- adapter_out: bfloat16 [8, 128, 3072], P('expert'), may hold values from -0.109375 to 0.109375
Outputs:
- input_grad: bfloat16 [768, 3072], P('expert', ('dp', 'tensor'))
- grad_in: float32 [8, 16384, 128], P('expert', ('dp', 'tensor'))
- grad_out: float32 [8, 128, 3072], P('expert', None, 'tensor')
The draws below stay inside these ranges and needn't reach their ends.
Inputs may be any that keep to these rules, and one draw needn't show every extreme that they name: `expert_ids`: the two experts of a token differ. Among the 96 tokens of each group (aligned blocks of the token rows of one index of expert), no expert is named more than 32 times, and in every draw some expert is named exactly 32 times in some group.
All inputs are finite; a program needn't handle non-finite values.
Results may differ from the reference program's by a relative error of at most 0.005.
Values may be sent and summed in bfloat16 or wider, within the bound.
No kernel may reach another device: no remote copies, remote signals or barrier semaphores. Data moves between devices by JAX's collectives and lax.ppermute only.
A program may use at most 32 MiB of HBM per device.

```python
import math
import jax
import jax.numpy as jnp
import numpy as np
from jax import lax

D = 3072
TEN = 8
RANK = 16
TOP = 2
CAP = 32
FF = 16384
EXPERTS = 8
TOKG = 96
TOKENS = 768
N_EXPERT = 8


def with_ends(result, stream_key, smallest, largest):
    index_at = [jax.random.randint(jax.random.fold_in(stream_key, axis), (), 0, length) for axis, length in enumerate(result.shape)]
    main_axis = result.shape.index(max(result.shape))
    neighbour = index_at[:main_axis] + [(index_at[main_axis] + 1) % result.shape[main_axis]] + index_at[main_axis + 1:]
    return result.at[tuple(index_at)].set(smallest).at[tuple(neighbour)].set(largest)


def block_scale(key, dims, split, smallest, largest):
    gain = 1.0
    for dim, parts in split:
        heights = jax.random.uniform(jax.random.fold_in(jax.random.fold_in(key, 6), dim), (parts,), jnp.float32, smallest / len(split), largest / len(split))
        gain = gain * jnp.repeat(jnp.exp(heights), dims[dim] // parts).reshape((-1,) + (1,) * (len(dims) - 1 - dim))
    return gain


def assign_block(rng, own, number, rows, amount, top, most, skew):
    ranking = jax.random.permutation(rng, amount)
    packed, ordinary = shares(amount, rows * top, most, skew, True), shares(amount, rows * top, most, skew, False)
    places = jnp.arange(amount)

    def named(sizes, offset_by):
        used = int((sizes > 0).sum())
        fixed = max(1, used // 4)
        moved = fixed + (places - fixed + offset_by * (used - fixed)) % max(1, amount - fixed)
        return jnp.zeros((amount,), jnp.int32).at[ranking[jnp.where(places < fixed, places, moved)]].set(jnp.asarray(sizes, jnp.int32))

    sizes = jnp.where(number % 4 == 0, named(packed, number // 4), named(ordinary, number - number // 4 - 1))
    mixed = jax.random.permutation(jax.random.fold_in(own, 3), amount)
    donor, taker = mixed[0:amount // 2 * 2:2], mixed[1:amount // 2 * 2:2]
    margin = jnp.minimum(sizes[donor] - 1, most - sizes[taker]) // 2
    margin = jnp.where((donor == ranking[0]) | (taker == ranking[0]) | (sizes[taker] == 0), 0, jnp.maximum(margin, 0))
    moved = jax.random.randint(jax.random.fold_in(own, 4), (amount // 2,), 0, 1 << 20) % (margin + 1)
    sizes = sizes.at[donor].add(-moved).at[taker].add(moved)
    members = jnp.searchsorted(jnp.cumsum(sizes), jnp.arange(rows * top), side="right").astype(jnp.int32)
    listing = members.reshape(top, rows).T
    listing = listing[jax.random.permutation(jax.random.fold_in(own, 1), rows)]
    offset_by = jax.random.randint(jax.random.fold_in(own, 2), (rows, 1), 0, top)
    return jnp.take_along_axis(listing, (jnp.arange(top)[None, :] + offset_by) % top, axis=1)


def shares(amount, total, most, skew, full):
    weights = [(1 << 20) // math.isqrt(grade ** skew) + 1 for grade in range(1, amount + 1)]
    largest = most if full else min(most, max(-(-total // amount), total * weights[0] // sum(weights)))
    least = 1 if total - largest >= amount - 1 else 0
    given, surplus = [largest] + [least] * (amount - 1), total - largest - least * (amount - 1)
    while surplus > 0:
        candidates = [i for i in range(1, amount) if given[i] < largest] or [i for i in range(1, amount) if given[i] < most]
        pool, remaining = sum([weights[i] for i in candidates]), surplus
        for i in candidates:
            addition = min(most - given[i], max(1, remaining * weights[i] // pool), surplus)
            given[i] = given[i] + addition
            surplus = surplus - addition
    return np.array(given)


def scatter_about(own_key, shape, width, most, pieces=(), kind=jnp.bfloat16):
    result = jax.random.normal(own_key, shape, jnp.float32) * width
    if len(pieces) > 0:
        result = block_scale(own_key, shape, pieces, -0.22, 0.18) * result
    return jnp.clip(result, min=-most, max=most).astype(kind)


def setup_inputs(seed: int = 0) -> dict:
    splits = jax.random.split(jax.random.key(seed), 11)
    tokens = scatter_about(splits[0], (TOKENS, D), 1.0, 6.0, ((0, 8), (1, 8)))
    cotangent = scatter_about(splits[1], (TOKENS, D), 1.0, 6.0, ((0, 8), (1, 8)))
    expert_ids_keys = jax.random.split(jax.random.fold_in(splits[2], 1), TOKENS // TOKG)
    expert_ids_turns = jax.random.permutation(jax.random.fold_in(splits[2], 3), TOKENS // TOKG)
    expert_ids = jax.vmap(lambda own, number: assign_block(jax.random.fold_in(splits[2], 2), own, number, TOKG, EXPERTS, TOP, CAP, 2))(expert_ids_keys, expert_ids_turns).reshape((TOKENS, TOP))
    gate_probs = jnp.clip(0.049804688 + 0.89941406 * jax.random.uniform(splits[3], (TOKENS, TOP), jnp.float32) ** block_scale(splits[3], (TOKENS, TOP), ((0, 8),), -0.2, 0.2), 0.049804688, 0.94921875).astype(jnp.bfloat16)
    tenant_ids = with_ends(jax.random.randint(splits[4], (TOKENS,), 0, TEN), jax.random.fold_in(splits[4], 1), 0, TEN - 1).astype(jnp.int32)
    w_gate = scatter_about(splits[5], (EXPERTS, D, FF), D ** -0.5, 0.109375, ((0, 8), (2, 128)))
    w_up = scatter_about(splits[6], (EXPERTS, D, FF), D ** -0.5, 0.109375, ((0, 8), (2, 128)))
    w_down = scatter_about(splits[7], (EXPERTS, FF, D), FF ** -0.5, 0.046875, ((0, 8), (1, 128)))
    adapter_in = scatter_about(splits[8], (EXPERTS, FF, TEN * RANK), FF ** -0.5, 0.046875, ((0, 8), (1, 128)))
    adapter_out = scatter_about(splits[9], (EXPERTS, TEN * RANK, D), D ** -0.5, 0.109375, ((0, 8),))
    return {"tokens": tokens, "cotangent": cotangent, "expert_ids": expert_ids, "gate_probs": gate_probs, "tenant_ids": tenant_ids, "w_gate": w_gate, "w_up": w_up, "w_down": w_down, "adapter_in": adapter_in, "adapter_out": adapter_out}


adapter_scale_factor = 2.0


def reference(tokens, cotangent, expert_ids, gate_probs, tenant_ids, w_gate, w_up, w_down, adapter_in, adapter_out):
    groups = N_EXPERT
    slot_count = N_EXPERT * CAP
    route_ids = expert_ids.reshape(groups, TOKG * TOP)
    onehot = (route_ids[:, :, None] == jnp.arange(EXPERTS, dtype=jnp.int32)[None, None, :]).astype(jnp.int32)
    earlier = jnp.cumsum(onehot, axis=1) - onehot
    slot_index = jnp.sum(earlier * onehot, axis=2)
    group_index = jnp.arange(groups, dtype=jnp.int32)[:, None]
    row_index = (group_index * CAP + slot_index).astype(jnp.int32)
    token_index = (group_index * TOKG + jnp.arange(TOKG * TOP, dtype=jnp.int32)[None, :] // TOP).astype(jnp.int32)
    inputs = jnp.zeros((EXPERTS, slot_count, D), jnp.bfloat16).at[route_ids, row_index].set(tokens[token_index])
    grads = jnp.zeros((EXPERTS, slot_count, D), jnp.bfloat16).at[route_ids, row_index].set(cotangent[token_index])
    weights = jnp.zeros((EXPERTS, slot_count), jnp.float32).at[route_ids, row_index].set(
        gate_probs.reshape(groups, TOKG * TOP).astype(jnp.float32))
    tenants = jnp.zeros((EXPERTS, slot_count), jnp.int32).at[route_ids, row_index].set(tenant_ids[token_index])
    column_tenant = jnp.arange(TEN * RANK, dtype=jnp.int32) // RANK

    def per_expert(items):
        x_rows, y_rows, weight_rows_matrix, t_rows, wg, wu, wd, a_in, a_out = items
        gate_val = jnp.dot(x_rows, wg, preferred_element_type=jnp.float32)
        up_val = jnp.dot(x_rows, wu, preferred_element_type=jnp.float32)
        sig = jax.nn.sigmoid(gate_val)
        silu_val = gate_val * sig
        hidden = (silu_val * up_val).astype(jnp.bfloat16)
        low_in = jnp.dot(hidden, a_in, preferred_element_type=jnp.float32)
        low_back = lax.dot_general(y_rows, a_out, (((1,), (1,)), ((), ())), preferred_element_type=jnp.float32)
        routing_flags = (t_rows[:, None] == column_tenant[None, :]).astype(jnp.float32)
        gate_weighted_rows = adapter_scale_factor * weight_rows_matrix[:, None] * routing_flags
        down_coef = (gate_weighted_rows * low_back).astype(jnp.bfloat16)
        up_coef = (gate_weighted_rows * low_in).astype(jnp.bfloat16)
        back = lax.dot_general(y_rows, wd, (((1,), (1,)), ((), ())), preferred_element_type=jnp.float32)
        hidden_gradient = weight_rows_matrix[:, None] * back + lax.dot_general(
            down_coef, a_in, (((1,), (1,)), ((), ())), preferred_element_type=jnp.float32)
        slope = sig * (1.0 + gate_val * (1.0 - sig))
        gate_grad = (hidden_gradient * up_val * slope).astype(jnp.bfloat16)
        up_grad = (hidden_gradient * silu_val).astype(jnp.bfloat16)
        row_grad = lax.dot_general(gate_grad, wg, (((1,), (1,)), ((), ())), preferred_element_type=jnp.float32)
        row_grad = row_grad + lax.dot_general(up_grad, wu, (((1,), (1,)), ((), ())), preferred_element_type=jnp.float32)
        grad_a = lax.dot_general(hidden, down_coef, (((0,), (0,)), ((), ())), preferred_element_type=jnp.float32)
        grad_b = lax.dot_general(up_coef, y_rows, (((0,), (0,)), ((), ())), preferred_element_type=jnp.float32)
        return row_grad, grad_a, grad_b

    row_grads, grad_in, grad_out = lax.map(
        per_expert, (inputs, grads, weights, tenants, w_gate, w_up, w_down, adapter_in, adapter_out))
    routed = row_grads[route_ids, row_index].reshape(groups, TOKG, TOP, D)
    total = routed[:, :, 0, :]
    for second in range(1, TOP):
        total = total + routed[:, :, second, :]
    input_grad = total.reshape(TOKENS, D).astype(jnp.bfloat16)
    return input_grad, grad_in, grad_out
```

```python
import jax
import jax.numpy as jnp
from jax import lax
from jax.sharding import Mesh, PartitionSpec as P

TEN = 8
RANK = 16
CAP = 32
SCALE = 2.0
BF = jnp.bfloat16
F32 = jnp.float32


def dot(a, b, ca, cb, precision=None):
    return lax.dot_general(
        a, b, (((ca,), (cb,)), ((), ())), precision=precision, preferred_element_type=F32
    )


def hot(index, size):
    return lax.broadcasted_iota(jnp.int32, (index.shape[0], size), 1) == index


def on_device(
    tokens,
    cotangent,
    expert_ids,
    gate_probs,
    tenant_ids,
    w_gate,
    w_up,
    w_down,
    adapter_in,
    adapter_out,
):
    nz, nx, ne, ny, nc = (lax.axis_size(a) for a in ("zh", "x", "e", "y", "c"))
    nxy = nx * ny
    group, width = tokens.shape
    slots = ne * CAP
    part = CAP // nx
    me_x, me_e, me_y, me_c = (lax.axis_index(a) for a in ("x", "e", "y", "c"))
    swap = [(0, 1), (1, 0)]
    gate_mat, up_mat, down_mat = w_gate[0], w_up[0], w_down[0]
    first, second = adapter_in[0], adapter_out[0]
    features = gate_mat.shape[0]
    piece = features // (nz * nxy * nc)

    named = [hot(expert_ids[:, j : j + 1], ne) for j in range(2)]
    either = (named[0] | named[1]).astype(BF)
    before = (
        lax.broadcasted_iota(jnp.int32, (group, group), 1)
        < lax.broadcasted_iota(jnp.int32, (group, group), 0)
    ).astype(BF)
    earlier = dot(before, either, 1, 0)
    slot = [
        jnp.sum(jnp.where(n, earlier, 0.0), axis=1, keepdims=True).astype(jnp.int32) for n in named
    ]
    tenant = tenant_ids[:, None]

    pick, marks, combine = None, None, None
    for j in range(2):
        expert = expert_ids[:, j : j + 1]
        quarter, rest = slot[j] // part, slot[j] % part
        here = hot(expert * part + rest, ne * part)
        mine = (here & (quarter == me_x)).astype(BF)
        weighted = here.astype(BF) * gate_probs[:, j : j + 1]
        mark = dot(weighted, hot(quarter * TEN + tenant, nx * TEN).astype(BF), 0, 0)
        back = hot(expert * CAP + slot[j], slots).astype(F32)
        pick = mine if pick is None else pick + mine
        marks = mark if marks is None else marks + mark
        combine = back if combine is None else combine + back
    rows = dot(pick, jnp.concatenate([tokens, cotangent], axis=1), 0, 0).astype(BF)
    pad = -(nx * TEN) % 128
    send = jnp.concatenate([rows, jnp.pad(marks.astype(BF), ((0, 0), (0, pad)))], axis=1)
    held = lax.all_to_all(
        send.reshape(ne, part, -1), "e", split_axis=0, concat_axis=0, tiled=True
    ).reshape(ne * part, -1)

    quarter_rows = ne * part
    block = held[:, : 2 * width]
    own = lax.all_to_all(
        jnp.broadcast_to(block[None], (nxy, quarter_rows, 2 * width)),
        ("y", "x"),
        split_axis=0,
        concat_axis=0,
        tiled=True,
    )
    other = lax.ppermute(own, "c", swap)
    low_core, high_core = jnp.where(me_c == 0, own, other), jnp.where(me_c == 0, other, own)
    both = jnp.stack([low_core, high_core]).reshape(nc, ny, nx, quarter_rows, 2, width)
    both = both.transpose(4, 2, 3, 1, 0, 5).reshape(2, slots, features)
    x_rows, y_rows = both[0], both[1]
    row_marks = held[:, 2 * width : 2 * width + nx * TEN].reshape(quarter_rows, nx, TEN)
    row_marks = row_marks.transpose(1, 0, 2).reshape(slots, TEN)
    column_of = lax.broadcasted_iota(jnp.int32, (TEN, TEN * RANK), 1) // RANK
    spread = (column_of == lax.broadcasted_iota(jnp.int32, (TEN, TEN * RANK), 0)).astype(BF)
    flags = dot(row_marks, spread, 1, 0)
    row_weight = jnp.sum(row_marks.astype(F32), axis=1, keepdims=True)

    gate_acc = dot(x_rows, gate_mat, 1, 0)
    up_acc = dot(x_rows, up_mat, 1, 0)
    back_acc = dot(y_rows, down_mat, 1, 1)
    low_back = dot(y_rows, second, 1, 1)
    sig = jax.nn.sigmoid(gate_acc)
    silu = gate_acc * sig
    hidden = (silu * up_acc).astype(BF)
    low_part = dot(hidden, first, 1, 0)
    down_coef = (SCALE * flags * low_back).astype(BF)
    hidden_grad = row_weight * back_acc + dot(down_coef, first, 1, 1)
    slope = sig * (1.0 + gate_acc * (1.0 - sig))
    gate_grad = (hidden_grad * up_acc * slope).astype(BF)
    up_grad = (hidden_grad * silu).astype(BF)
    grad_a = dot(hidden, down_coef, 0, 0)

    rank_of = lax.broadcasted_iota(jnp.int32, (TEN * RANK, RANK), 0) % RANK
    fold = (rank_of == lax.broadcasted_iota(jnp.int32, (TEN * RANK, RANK), 1)).astype(BF)
    kept = jnp.where(flags != 0.0, low_part, 0.0).astype(BF)
    low_rows = dot(fold, kept, 0, 1).astype(BF)
    term = dot(gate_mat, gate_grad, 1, 1) + dot(up_mat, up_grad, 1, 1)
    term = term.astype(BF).reshape(nz, nxy, nc, piece, slots).transpose(2, 1, 0, 3, 4)
    term = term.reshape(nc, nxy, nz * piece, slots)
    extra = jnp.pad(low_rows[:, None, :], ((0, 0), (0, 7), (0, 0)))
    term = jnp.concatenate([term, jnp.broadcast_to(extra[None], (nc,) + extra.shape)], axis=2)
    keep = lax.dynamic_index_in_dim(term, me_c, 0, keepdims=False)
    give = lax.dynamic_index_in_dim(term, 1 - me_c, 0, keepdims=False)
    pair = (keep.astype(F32) + lax.ppermute(give, "c", swap).astype(F32)).astype(BF)
    plane = lax.all_to_all(pair, ("x", "y"), split_axis=0, concat_axis=0, tiled=True)
    plane = jnp.sum(plane.astype(F32), axis=0).astype(BF)

    feats = plane[: nz * piece].reshape(nz, piece, nx, ne, part).transpose(0, 3, 1, 2, 4)
    lanes = 128
    feats = feats.reshape(nz * ne, piece * CAP // lanes, lanes)
    low_line = plane[nz * piece].reshape(1, slots // lanes, lanes)
    outgoing = jnp.concatenate(
        [feats, jnp.broadcast_to(low_line, (nz * ne, slots // lanes, lanes))], axis=1
    )
    came = lax.all_to_all(outgoing, ("zh", "e"), split_axis=0, concat_axis=0, tiled=True)
    came = came.reshape(nz, ne, -1, lanes)
    n_feat = piece * CAP // lanes
    total = jnp.sum(came.astype(F32), axis=0)
    returned = total[:, :n_feat].reshape(ne, piece, CAP).transpose(1, 0, 2).reshape(piece, slots)
    input_grad = dot(combine, returned, 1, 1, lax.Precision.HIGHEST).astype(BF)

    low_mine = lax.dynamic_index_in_dim(total, me_e, 0, keepdims=False)[n_feat:]
    low_all = lax.all_gather(low_mine, ("x", "y"), axis=0, tiled=False).reshape(RANK, slots)
    tiled = jnp.tile(low_all, (TEN, 1))
    up_coef = (SCALE * flags * tiled.T).astype(BF)
    local = lax.dynamic_index_in_dim(
        own.reshape(ny, nx * quarter_rows, 2 * width), me_y, 0, keepdims=False
    )[:, width:]
    grad_b = dot(up_coef, local, 0, 0)
    return input_grad, grad_a[None], grad_b[None]


def solution(mesh):
    tensor, dp, expert = mesh.shape["tensor"], mesh.shape["dp"], mesh.shape["expert"]
    fine = Mesh(
        mesh.devices.reshape(dp // 4, 4, expert, tensor // 2, 2), ("zh", "x", "e", "y", "c")
    )
    units, cols = ("zh", "x", "y", "c"), ("y", "c")
    return jax.shard_map(
        on_device,
        mesh=fine,
        in_specs=(
            P("e", cols),
            P("e", cols),
            P("e", None),
            P("e", None),
            P("e"),
            P("e", None, units),
            P("e", None, units),
            P("e", units, None),
            P("e", units, None),
            P("e", None, None),
        ),
        out_specs=(P("e", units), P("e", units, None), P("e", None, cols)),
        check_vma=False,
    )
```

```python
import functools

import jax
import jax.numpy as jnp
from jax import lax
from jax.experimental import pallas as pl
from jax.experimental.pallas import tpu as pltpu
from jax.sharding import Mesh, PartitionSpec as P

TEN = 8
RANK = 16
CAP = 32
SCALE = 2.0
BF = jnp.bfloat16
F32 = jnp.float32


def dot(a, b, ca, cb, precision=None):
    return lax.dot_general(
        a, b, (((ca,), (cb,)), ((), ())), precision=precision, preferred_element_type=F32
    )


def hot(index, size):
    return lax.broadcasted_iota(jnp.int32, (index.shape[0], size), 1) == index


def expert_kernel(
    sizes, core, own, other, held_marks, gate_mat, up_mat, down_mat, first, second,
    keep, give, hidden_out, down_out, flags_out, terms,
):
    nz, nx, ny, nc = sizes
    nxy = nx * ny
    mine = core[0]
    quarter_rows, width = own.shape[1], own.shape[2] // 2
    slots = nx * quarter_rows
    features = gate_mat.shape[0]
    part, piece = features // nz, features // (nz * nxy * nc)
    low_width = first.shape[1]

    forward, backward = None, None
    for y in range(ny):
        for ref, at_core in ((own, mine), (other, 1 - mine)):
            at = pl.multiple_of((y * nc + at_core) * width, 128)
            both = ref[y * nx : (y + 1) * nx].reshape(slots, 2 * width)
            mats = jnp.concatenate([gate_mat[pl.ds(at, width), :], up_mat[pl.ds(at, width), :]], 1)
            ahead = dot(both[:, :width], mats, 1, 0)
            mats = jnp.concatenate([down_mat[:, pl.ds(at, width)], second[:, pl.ds(at, width)]], 0)
            behind = dot(both[:, width:], mats, 1, 1)
            forward = ahead if forward is None else forward + ahead
            backward = behind if backward is None else backward + behind
    units = gate_mat.shape[1]
    gate_acc, up_acc = forward[:, :units], forward[:, units:]
    back_acc, low_back = backward[:, :units], backward[:, units:]

    mark_rows = held_marks[...]
    lane = lax.broadcasted_iota(jnp.int32, (mark_rows.shape[1], low_width), 0)
    tenant_of = lax.broadcasted_iota(jnp.int32, (mark_rows.shape[1], low_width), 1) // RANK
    flags, weight = [], []
    for x in range(nx):
        flags.append(dot(mark_rows, (lane == x * TEN + tenant_of).astype(BF), 1, 0))
        inside = (lane >= x * TEN) & (lane < (x + 1) * TEN)
        weight.append(dot(mark_rows, inside.astype(BF), 1, 0))
    flags, weight = jnp.concatenate(flags, 0), jnp.concatenate(weight, 0)[:, :1]

    sig = jax.nn.sigmoid(gate_acc)
    silu = gate_acc * sig
    hidden = (silu * up_acc).astype(BF)
    low_part = dot(hidden, first[...], 1, 0)
    down_coef = (SCALE * flags * low_back).astype(BF)
    hidden_grad = weight * back_acc + dot(down_coef, first[...], 1, 1)
    slope = sig * (1.0 + gate_acc * (1.0 - sig))
    gate_grad = (hidden_grad * up_acc * slope).astype(BF)
    up_grad = (hidden_grad * silu).astype(BF)
    hidden_out[...] = hidden
    down_out[...] = down_coef
    flags_out[...] = flags

    grads = jnp.concatenate([gate_grad, up_grad], 1)
    for z in range(nz):
        at = slice(z * part, (z + 1) * part)
        mats = jnp.concatenate([gate_mat[at, :], up_mat[at, :]], 1)
        terms[at, :] = dot(mats, grads, 1, 1)

    rank_of = lax.broadcasted_iota(jnp.int32, (RANK, low_width), 1) % RANK
    fold = (rank_of == lax.broadcasted_iota(jnp.int32, (RANK, low_width), 0)).astype(BF)
    kept = jnp.where(flags != 0.0, low_part, 0.0).astype(BF)
    low_rows = dot(fold, kept, 1, 1)
    under = lax.broadcasted_iota(jnp.int32, (16, slots), 0) == 0
    for p in range(nxy):
        for out, at_core in ((keep, mine), (give, 1 - mine)):
            chunks = [
                terms[pl.ds(pl.multiple_of(z * part + (p * nc + at_core) * piece, 8), piece), :]
                for z in range(nz)
            ]
            chunks.append(jnp.where(under, low_rows[p : p + 1, :], 0.0))
            out[p] = jnp.concatenate(chunks, 0).astype(out.dtype)


def on_device(
    tokens,
    cotangent,
    expert_ids,
    gate_probs,
    tenant_ids,
    w_gate,
    w_up,
    w_down,
    adapter_in,
    adapter_out,
):
    nz, nx, ne, ny, nc = (lax.axis_size(a) for a in ("zh", "x", "e", "y", "c"))
    nxy = nx * ny
    group, width = tokens.shape
    slots = ne * CAP
    part = CAP // nx
    me_x, me_e, me_y, me_c = (lax.axis_index(a) for a in ("x", "e", "y", "c"))
    swap = [(0, 1), (1, 0)]
    gate_mat, up_mat, down_mat = w_gate[0], w_up[0], w_down[0]
    first, second = adapter_in[0], adapter_out[0]
    features = gate_mat.shape[0]
    piece = features // (nz * nxy * nc)

    named = [hot(expert_ids[:, j : j + 1], ne) for j in range(2)]
    either = (named[0] | named[1]).astype(BF)
    before = (
        lax.broadcasted_iota(jnp.int32, (group, group), 1)
        < lax.broadcasted_iota(jnp.int32, (group, group), 0)
    ).astype(BF)
    earlier = dot(before, either, 1, 0)
    slot = [
        jnp.sum(jnp.where(n, earlier, 0.0), axis=1, keepdims=True).astype(jnp.int32) for n in named
    ]
    tenant = tenant_ids[:, None]

    pick, marks, combine = None, None, None
    for j in range(2):
        expert = expert_ids[:, j : j + 1]
        quarter, rest = slot[j] // part, slot[j] % part
        here = hot(expert * part + rest, ne * part)
        mine = (here & (quarter == me_x)).astype(BF)
        weighted = here.astype(BF) * gate_probs[:, j : j + 1]
        mark = dot(weighted, hot(quarter * TEN + tenant, nx * TEN).astype(BF), 0, 0)
        back = hot(expert * CAP + slot[j], slots).astype(F32)
        pick = mine if pick is None else pick + mine
        marks = mark if marks is None else marks + mark
        combine = back if combine is None else combine + back
    rows = dot(pick, jnp.concatenate([tokens, cotangent], axis=1), 0, 0).astype(BF)
    pad = -(nx * TEN) % 128
    send = jnp.concatenate([rows, jnp.pad(marks.astype(BF), ((0, 0), (0, pad)))], axis=1)
    held = lax.all_to_all(
        send.reshape(ne, part, -1), "e", split_axis=0, concat_axis=0, tiled=True
    ).reshape(ne * part, -1)

    quarter_rows = ne * part
    block = held[:, : 2 * width]
    own = lax.all_to_all(
        jnp.broadcast_to(block[None], (nxy, quarter_rows, 2 * width)),
        ("y", "x"),
        split_axis=0,
        concat_axis=0,
        tiled=True,
    )
    other = lax.ppermute(own, "c", swap)
    units, low_width = gate_mat.shape[1], first.shape[1]
    tall = nz * piece + 16
    in_vmem = pl.BlockSpec(memory_space=pltpu.VMEM)
    keep, give, hidden, down_coef, flags = pl.pallas_call(
        functools.partial(expert_kernel, (nz, nx, ny, nc)),
        out_shape=(
            jax.ShapeDtypeStruct((nxy, tall, slots), F32),
            jax.ShapeDtypeStruct((nxy, tall, slots), BF),
            jax.ShapeDtypeStruct((slots, units), BF),
            jax.ShapeDtypeStruct((slots, low_width), BF),
            jax.ShapeDtypeStruct((slots, low_width), F32),
        ),
        in_specs=[pl.BlockSpec(memory_space=pltpu.SMEM)] + [in_vmem] * 8,
        out_specs=(in_vmem,) * 5,
        scratch_shapes=[pltpu.VMEM((features, slots), F32)],
        compiler_params=pltpu.CompilerParams(vmem_limit_bytes=40 << 20),
        cost_estimate=pl.CostEstimate(
            flops=10 * slots * features * units, bytes_accessed=9 << 20, transcendentals=slots * units
        ),
    )(
        me_c.reshape(1).astype(jnp.int32),
        own,
        other,
        held[:, 2 * width :],
        gate_mat,
        up_mat,
        down_mat,
        first,
        second,
    )
    grad_a = dot(hidden, down_coef, 0, 0)
    pair = keep + lax.ppermute(give, "c", swap).astype(F32)
    pair = pair[:, : nz * piece + 8].astype(BF)
    plane = lax.all_to_all(pair, ("x", "y"), split_axis=0, concat_axis=0, tiled=True)
    plane = jnp.sum(plane.astype(F32), axis=0).astype(BF)

    feats = plane[: nz * piece].reshape(nz, piece, nx, ne, part).transpose(0, 3, 1, 2, 4)
    lanes = 128
    feats = feats.reshape(nz * ne, piece * CAP // lanes, lanes)
    low_line = plane[nz * piece].reshape(1, slots // lanes, lanes)
    outgoing = jnp.concatenate(
        [feats, jnp.broadcast_to(low_line, (nz * ne, slots // lanes, lanes))], axis=1
    )
    came = lax.all_to_all(outgoing, ("zh", "e"), split_axis=0, concat_axis=0, tiled=True)
    came = came.reshape(nz, ne, -1, lanes)
    n_feat = piece * CAP // lanes
    total = jnp.sum(came.astype(F32), axis=0)
    returned = total[:, :n_feat].reshape(ne, piece, CAP).transpose(1, 0, 2).reshape(piece, slots)
    input_grad = dot(combine, returned, 1, 1, lax.Precision.HIGHEST).astype(BF)

    low_mine = lax.dynamic_index_in_dim(total, me_e, 0, keepdims=False)[n_feat:]
    low_all = lax.all_to_all(
        jnp.broadcast_to(low_mine[None], (nxy,) + low_mine.shape),
        ("x", "y"),
        split_axis=0,
        concat_axis=0,
        tiled=True,
    ).reshape(RANK, slots)
    tiled = jnp.tile(low_all, (TEN, 1))
    up_coef = (SCALE * flags * tiled.T).astype(BF)
    local = lax.dynamic_index_in_dim(
        own.reshape(ny, nx * quarter_rows, 2 * width), me_y, 0, keepdims=False
    )[:, width:]
    grad_b = dot(up_coef, local, 0, 0)
    return input_grad, grad_a[None], grad_b[None]


def solution(mesh):
    tensor, dp, expert = mesh.shape["tensor"], mesh.shape["dp"], mesh.shape["expert"]
    fine = Mesh(
        mesh.devices.reshape(dp // 4, 4, expert, tensor // 2, 2), ("zh", "x", "e", "y", "c")
    )
    units, cols = ("zh", "x", "y", "c"), ("y", "c")
    return jax.shard_map(
        on_device,
        mesh=fine,
        in_specs=(
            P("e", cols),
            P("e", cols),
            P("e", None),
            P("e", None),
            P("e"),
            P("e", None, units),
            P("e", None, units),
            P("e", units, None),
            P("e", units, None),
            P("e", None, None),
        ),
        out_specs=(P("e", units), P("e", units, None), P("e", None, cols)),
        check_vma=False,
    )
```

```python
import functools

import jax
import jax.numpy as jnp
from jax import lax
from jax.experimental import pallas as pl
from jax.experimental.pallas import tpu as pltpu
from jax.sharding import Mesh, PartitionSpec as P

TEN = 8
RANK = 16
CAP = 32
SCALE = 2.0
BF = jnp.bfloat16
F32 = jnp.float32


def dot(a, b, ca, cb, precision=None):
    return lax.dot_general(
        a, b, (((ca,), (cb,)), ((), ())), precision=precision, preferred_element_type=F32
    )


def dispatch_kernel(nx, ne, where, ids, probs, tenants, tokens, cotangent, send, combine):
    group, width = tokens.shape
    part = CAP // nx
    shift = part.bit_length() - 1
    rank_in = functools.partial(lax.broadcasted_iota, jnp.int32)
    named = [rank_in((ne, group), 0) == ids[j : j + 1, :] for j in range(2)]
    either = (named[0] | named[1]).astype(F32).astype(BF)
    before = (rank_in((group, group), 0) < rank_in((group, group), 1)).astype(F32).astype(BF)
    earlier = dot(either, before, 1, 0)
    pick, marks, back = None, None, None
    for j in range(2):
        expert = ids[j : j + 1, :]
        slot = jnp.sum(jnp.where(named[j], earlier, 0.0), axis=0, keepdims=True).astype(jnp.int32)
        quarter, rest = slot >> shift, slot & (part - 1)
        here = rank_in((ne * part, group), 0) == expert * part + rest
        mine = jnp.where(here & (quarter == where[0]), 1.0, 0.0)
        weighted = jnp.where(here, probs[j : j + 1, :].astype(F32), 0.0).astype(BF)
        column = rank_in((128, group), 0) == quarter * TEN + tenants[...]
        mark = dot(weighted, jnp.where(column, 1.0, 0.0).astype(BF), 1, 1)
        home = jnp.where(rank_in((ne * CAP, group), 0) == expert * CAP + slot, 1.0, 0.0)
        pick = mine if pick is None else pick + mine
        marks = mark if marks is None else marks + mark
        back = home if back is None else back + home
    pick = pick.astype(BF)
    rows = [dot(pick, tokens[...], 1, 0), dot(pick, cotangent[...], 1, 0), marks]
    rows = jnp.concatenate(rows, 1).reshape(ne, part, 2 * width + 128)
    send[...] = rows.astype(BF)
    combine[...] = back


def expert_kernel(
    sizes, core, own, other, held_marks, gate_mat, up_mat, down_mat, first, second,
    keep, give, hidden_out, down_out, flags_out, terms,
):
    nz, nx, ny, nc, ne = sizes
    nxy = nx * ny
    mine = core[0]
    quarter_rows, width = own.shape[1], own.shape[2] // 2
    slots = nx * quarter_rows
    features = gate_mat.shape[0]
    part, piece = features // nz, features // (nz * nxy * nc)
    low_width = first.shape[1]

    forward, backward = None, None
    for y in range(ny):
        for ref, at_core in ((own, mine), (other, 1 - mine)):
            at = pl.multiple_of((y * nc + at_core) * width, 128)
            both = ref[y * nx : (y + 1) * nx].reshape(slots, 2 * width)
            mats = jnp.concatenate([gate_mat[pl.ds(at, width), :], up_mat[pl.ds(at, width), :]], 1)
            ahead = dot(both[:, :width], mats, 1, 0)
            mats = jnp.concatenate([down_mat[:, pl.ds(at, width)], second[:, pl.ds(at, width)]], 0)
            behind = dot(both[:, width:], mats, 1, 1)
            forward = ahead if forward is None else forward + ahead
            backward = behind if backward is None else backward + behind
    units = gate_mat.shape[1]
    gate_acc, up_acc = forward[:, :units], forward[:, units:]
    back_acc, low_back = backward[:, :units], backward[:, units:]

    mark_rows = held_marks[...]
    lane = lax.broadcasted_iota(jnp.int32, (mark_rows.shape[1], low_width), 0)
    tenant_of = lax.broadcasted_iota(jnp.int32, (mark_rows.shape[1], low_width), 1) // RANK
    flags, weight = [], []
    for x in range(nx):
        flags.append(dot(mark_rows, (lane == x * TEN + tenant_of).astype(BF), 1, 0))
        inside = (lane >= x * TEN) & (lane < (x + 1) * TEN)
        weight.append(dot(mark_rows, inside.astype(BF), 1, 0))
    flags, weight = jnp.concatenate(flags, 0), jnp.concatenate(weight, 0)[:, :1]

    sig = jax.nn.sigmoid(gate_acc)
    silu = gate_acc * sig
    hidden = (silu * up_acc).astype(BF)
    low_part = dot(hidden, first[...], 1, 0)
    down_coef = (SCALE * flags * low_back).astype(BF)
    hidden_grad = weight * back_acc + dot(down_coef, first[...], 1, 1)
    slope = sig * (1.0 + gate_acc * (1.0 - sig))
    gate_grad = hidden_grad * up_acc * slope
    up_grad = hidden_grad * silu
    hidden_out[...] = hidden
    down_out[...] = down_coef
    flags_out[...] = flags

    grads = jnp.concatenate([gate_grad, up_grad], 1)
    size = quarter_rows // ne
    starts = [x * quarter_rows + e * size for e in range(ne) for x in range(nx)]
    grads = jnp.concatenate([grads[at : at + size] for at in starts], 0).astype(BF)
    for z in range(nz):
        at = slice(z * part, (z + 1) * part)
        mats = jnp.concatenate([gate_mat[at, :], up_mat[at, :]], 1)
        terms[at, :] = dot(mats, grads, 1, 1)

    rank_of = lax.broadcasted_iota(jnp.int32, (RANK, low_width), 1) % RANK
    fold = (rank_of == lax.broadcasted_iota(jnp.int32, (RANK, low_width), 0)).astype(BF)
    kept = jnp.where(flags != 0.0, low_part, 0.0).astype(BF)
    low_rows = dot(fold, kept, 1, 1)
    for p in range(nxy):
        for out, at_core in ((keep, mine), (give, 1 - mine)):
            chunks = [
                terms[pl.ds(pl.multiple_of(z * part + (p * nc + at_core) * piece, 8), piece), :]
                for z in range(nz)
            ]
            chunks.append(low_rows)
            out[p] = jnp.concatenate(chunks, 0).astype(out.dtype)


def on_device(
    tokens,
    cotangent,
    expert_ids,
    gate_probs,
    tenant_ids,
    w_gate,
    w_up,
    w_down,
    adapter_in,
    adapter_out,
):
    nz, nx, ne, ny, nc = (lax.axis_size(a) for a in ("zh", "x", "e", "y", "c"))
    nxy = nx * ny
    group, width = tokens.shape
    slots = ne * CAP
    part = CAP // nx
    me_x, me_y, me_c = (lax.axis_index(a) for a in ("x", "y", "c"))
    swap = [(0, 1), (1, 0)]
    gate_mat, up_mat, down_mat = w_gate[0], w_up[0], w_down[0]
    first, second = adapter_in[0], adapter_out[0]
    features = gate_mat.shape[0]
    piece = features // (nz * nxy * nc)

    in_vmem = pl.BlockSpec(memory_space=pltpu.VMEM)
    in_smem = pl.BlockSpec(memory_space=pltpu.SMEM)
    send, combine = pl.pallas_call(
        functools.partial(dispatch_kernel, nx, ne),
        out_shape=(
            jax.ShapeDtypeStruct((ne, part, 2 * width + 128), BF),
            jax.ShapeDtypeStruct((slots, group), F32),
        ),
        in_specs=[in_smem] + [in_vmem] * 5,
        out_specs=(in_vmem,) * 2,
    )(
        me_x.reshape(1).astype(jnp.int32),
        expert_ids.T,
        gate_probs.T,
        tenant_ids[None],
        tokens,
        cotangent,
    )
    held = lax.all_to_all(send, "e", split_axis=0, concat_axis=0, tiled=True)
    held = held.reshape(ne * part, -1)

    quarter_rows = ne * part
    block = held[:, : 2 * width]
    own = lax.all_to_all(
        jnp.broadcast_to(block[None], (nxy, quarter_rows, 2 * width)),
        ("y", "x"),
        split_axis=0,
        concat_axis=0,
        tiled=True,
    )
    other = lax.ppermute(own, "c", swap)
    units, low_width = gate_mat.shape[1], first.shape[1]
    tall = nz * piece + RANK
    keep, give, hidden, down_coef, flags = pl.pallas_call(
        functools.partial(expert_kernel, (nz, nx, ny, nc, ne)),
        out_shape=(
            jax.ShapeDtypeStruct((nxy, tall, slots), F32),
            jax.ShapeDtypeStruct((nxy, tall, slots), BF),
            jax.ShapeDtypeStruct((slots, units), BF),
            jax.ShapeDtypeStruct((slots, low_width), BF),
            jax.ShapeDtypeStruct((slots, low_width), F32),
        ),
        in_specs=[in_smem] + [in_vmem] * 8,
        out_specs=(in_vmem,) * 5,
        scratch_shapes=[pltpu.VMEM((features, slots), F32)],
        compiler_params=pltpu.CompilerParams(vmem_limit_bytes=40 << 20),
        cost_estimate=pl.CostEstimate(
            flops=10 * slots * features * units, bytes_accessed=9 << 20, transcendentals=slots * units
        ),
    )(
        me_c.reshape(1).astype(jnp.int32),
        own,
        other,
        held[:, 2 * width :],
        gate_mat,
        up_mat,
        down_mat,
        first,
        second,
    )
    grad_a = dot(hidden, down_coef, 0, 0)
    pair = (keep + lax.ppermute(give, "c", swap).astype(F32)).astype(BF)
    plane = lax.all_to_all(pair, ("x", "y"), split_axis=0, concat_axis=0, tiled=True)
    plane = jnp.sum(plane.astype(F32), axis=0)

    def share(z):
        return jnp.concatenate(
            [lax.dynamic_slice_in_dim(plane, z * piece, piece, 0), plane[nz * piece :]], axis=0
        )

    me_z = lax.axis_index("zh")
    total = share(me_z)
    for k in sorted(range(1, nz), key=lambda k: -min(k, nz - k)):
        block = share((me_z + k) % nz).astype(BF)
        total += lax.ppermute(block, "zh", [(i, (i + k) % nz) for i in range(nz)]).astype(F32)

    lanes = 128
    feats = total[:piece].reshape(piece, ne, CAP).transpose(1, 0, 2)
    came = lax.all_to_all(
        feats.reshape(ne, piece * CAP // lanes, lanes),
        "e",
        split_axis=0,
        concat_axis=0,
        tiled=True,
    )
    returned = came.reshape(ne, piece, CAP).transpose(1, 0, 2).reshape(piece, slots)
    input_grad = dot(combine, returned, 0, 1, lax.Precision.HIGHEST).astype(BF)

    low_all = total[piece:]
    tiled = jnp.tile(low_all, (TEN, 1))
    up_coef = (SCALE * flags * tiled.T).astype(BF)
    local = lax.dynamic_index_in_dim(
        own.reshape(ny, nx * quarter_rows, 2 * width), me_y, 0, keepdims=False
    )[:, width:]
    grad_b = dot(up_coef, local, 0, 0)
    return input_grad, grad_a[None], grad_b[None]


def solution(mesh):
    tensor, dp, expert = mesh.shape["tensor"], mesh.shape["dp"], mesh.shape["expert"]
    fine = Mesh(
        mesh.devices.reshape(dp // 4, 4, expert, tensor // 2, 2), ("zh", "x", "e", "y", "c")
    )
    units, cols = ("zh", "x", "y", "c"), ("y", "c")
    return jax.shard_map(
        on_device,
        mesh=fine,
        in_specs=(
            P("e", cols),
            P("e", cols),
            P("e", None),
            P("e", None),
            P("e"),
            P("e", None, units),
            P("e", None, units),
            P("e", units, None),
            P("e", units, None),
            P("e", None, None),
        ),
        out_specs=(P("e", units), P("e", units, None), P("e", None, cols)),
        check_vma=False,
    )
```

```python
import functools

import jax
import jax.numpy as jnp
from jax import lax
from jax.experimental import pallas as pl
from jax.experimental.pallas import tpu as pltpu
from jax.sharding import Mesh, PartitionSpec as P

TEN = 8
RANK = 16
CAP = 32
SCALE = 2.0
BF = jnp.bfloat16
F32 = jnp.float32


def dot(a, b, ca, cb, precision=None):
    return lax.dot_general(
        a, b, (((ca,), (cb,)), ((), ())), precision=precision, preferred_element_type=F32
    )


def dispatch_kernel(nx, ne, where, ids, probs, tenants, tokens, cotangent, send, combine):
    group, width = tokens.shape
    part = CAP // nx
    shift = part.bit_length() - 1
    rank_in = functools.partial(lax.broadcasted_iota, jnp.int32)
    named = [rank_in((ne, group), 0) == ids[j : j + 1, :] for j in range(2)]
    either = (named[0] | named[1]).astype(F32).astype(BF)
    before = (rank_in((group, group), 0) < rank_in((group, group), 1)).astype(F32).astype(BF)
    earlier = dot(either, before, 1, 0)
    pick, marks, back = None, None, None
    for j in range(2):
        expert = ids[j : j + 1, :]
        slot = jnp.sum(jnp.where(named[j], earlier, 0.0), axis=0, keepdims=True).astype(jnp.int32)
        quarter, rest = slot >> shift, slot & (part - 1)
        here = rank_in((ne * part, group), 0) == expert * part + rest
        mine = jnp.where(here & (quarter == where[0]), 1.0, 0.0)
        weighted = jnp.where(here, probs[j : j + 1, :].astype(F32), 0.0).astype(BF)
        column = rank_in((128, group), 0) == quarter * TEN + tenants[...]
        mark = dot(weighted, jnp.where(column, 1.0, 0.0).astype(BF), 1, 1)
        home = jnp.where(rank_in((ne * CAP, group), 0) == expert * CAP + slot, 1.0, 0.0)
        pick = mine if pick is None else pick + mine
        marks = mark if marks is None else marks + mark
        back = home if back is None else back + home
    pick = pick.astype(BF)
    rows = [dot(pick, tokens[...], 1, 0), dot(pick, cotangent[...], 1, 0), marks]
    rows = jnp.concatenate(rows, 1).reshape(ne, part, 2 * width + 128)
    send[...] = rows.astype(BF)
    combine[...] = back


def expert_kernel(
    sizes, core, own, other, held_marks, gate_mat, up_mat, down_mat, first, second,
    keep, give, hidden_out, down_out, flags_out, terms,
):
    nz, nx, ny, nc, ne = sizes
    nxy = nx * ny
    mine = core[0]
    quarter_rows, width = own.shape[1], own.shape[2] // 2
    slots = nx * quarter_rows
    features = gate_mat.shape[0]
    part, piece = features // nz, features // (nz * nxy * nc)
    low_width = first.shape[1]

    forward, backward = None, None
    for y in range(ny):
        for ref, at_core in ((own, mine), (other, 1 - mine)):
            at = pl.multiple_of((y * nc + at_core) * width, 128)
            both = ref[y * nx : (y + 1) * nx].reshape(slots, 2 * width)
            mats = jnp.concatenate([gate_mat[pl.ds(at, width), :], up_mat[pl.ds(at, width), :]], 1)
            ahead = dot(both[:, :width], mats, 1, 0)
            mats = jnp.concatenate([down_mat[:, pl.ds(at, width)], second[:, pl.ds(at, width)]], 0)
            behind = dot(both[:, width:], mats, 1, 1)
            forward = ahead if forward is None else forward + ahead
            backward = behind if backward is None else backward + behind
    units = gate_mat.shape[1]
    gate_acc, up_acc = forward[:, :units], forward[:, units:]
    back_acc, low_back = backward[:, :units], backward[:, units:]

    mark_rows = held_marks[...]
    lane = lax.broadcasted_iota(jnp.int32, (mark_rows.shape[1], low_width), 0)
    tenant_of = lax.broadcasted_iota(jnp.int32, (mark_rows.shape[1], low_width), 1) // RANK
    flags, weight = [], []
    for x in range(nx):
        flags.append(dot(mark_rows, (lane == x * TEN + tenant_of).astype(BF), 1, 0))
        inside = (lane >= x * TEN) & (lane < (x + 1) * TEN)
        weight.append(dot(mark_rows, inside.astype(BF), 1, 0))
    flags, weight = jnp.concatenate(flags, 0), jnp.concatenate(weight, 0)[:, :1]

    sig = jax.nn.sigmoid(gate_acc)
    silu = gate_acc * sig
    hidden = (silu * up_acc).astype(BF)
    low_part = dot(hidden, first[...], 1, 0)
    down_coef = (SCALE * flags * low_back).astype(BF)
    hidden_grad = weight * back_acc + dot(down_coef, first[...], 1, 1)
    slope = sig * (1.0 + gate_acc * (1.0 - sig))
    gate_grad = hidden_grad * up_acc * slope
    up_grad = hidden_grad * silu
    hidden_out[...] = hidden
    down_out[...] = down_coef
    flags_out[...] = flags

    grads = jnp.concatenate([gate_grad, up_grad], 1)
    size = quarter_rows // ne
    starts = [x * quarter_rows + e * size for e in range(ne) for x in range(nx)]
    grads = jnp.concatenate([grads[at : at + size] for at in starts], 0).astype(BF)
    for z in range(nz):
        at = slice(z * part, (z + 1) * part)
        mats = jnp.concatenate([gate_mat[at, :], up_mat[at, :]], 1)
        terms[at, :] = dot(mats, grads, 1, 1)

    rank_of = lax.broadcasted_iota(jnp.int32, (RANK, low_width), 1) % RANK
    fold = (rank_of == lax.broadcasted_iota(jnp.int32, (RANK, low_width), 0)).astype(BF)
    kept = jnp.where(flags != 0.0, low_part, 0.0).astype(BF)
    low_rows = dot(fold, kept, 1, 1)
    for p in range(nxy):
        for out, at_core in ((keep, mine), (give, 1 - mine)):
            chunks = [
                terms[pl.ds(pl.multiple_of(z * part + (p * nc + at_core) * piece, 8), piece), :]
                for z in range(nz)
            ]
            chunks.append(low_rows)
            out[p] = jnp.concatenate(chunks, 0).astype(out.dtype)


def on_device(
    tokens,
    cotangent,
    expert_ids,
    gate_probs,
    tenant_ids,
    w_gate,
    w_up,
    w_down,
    adapter_in,
    adapter_out,
):
    nz, nx, ne, ny, nc = (lax.axis_size(a) for a in ("zh", "x", "e", "y", "c"))
    nxy = nx * ny
    group, width = tokens.shape
    slots = ne * CAP
    part = CAP // nx
    me_x, me_y, me_c = (lax.axis_index(a) for a in ("x", "y", "c"))
    swap = [(0, 1), (1, 0)]
    gate_mat, up_mat, down_mat = w_gate[0], w_up[0], w_down[0]
    first, second = adapter_in[0], adapter_out[0]
    features = gate_mat.shape[0]
    piece = features // (nz * nxy * nc)

    in_vmem = pl.BlockSpec(memory_space=pltpu.VMEM)
    in_smem = pl.BlockSpec(memory_space=pltpu.SMEM)
    send, combine = pl.pallas_call(
        functools.partial(dispatch_kernel, nx, ne),
        out_shape=(
            jax.ShapeDtypeStruct((ne, part, 2 * width + 128), BF),
            jax.ShapeDtypeStruct((slots, group), F32),
        ),
        in_specs=[in_smem] + [in_vmem] * 5,
        out_specs=(in_vmem,) * 2,
    )(
        me_x.reshape(1).astype(jnp.int32),
        expert_ids.T,
        gate_probs.T,
        tenant_ids[None],
        tokens,
        cotangent,
    )
    held = lax.all_to_all(send, "e", split_axis=0, concat_axis=0, tiled=True)
    held = held.reshape(ne * part, -1)

    quarter_rows = ne * part
    block = held[:, : 2 * width]
    own = lax.all_to_all(
        jnp.broadcast_to(block[None], (nxy, quarter_rows, 2 * width)),
        ("y", "x"),
        split_axis=0,
        concat_axis=0,
        tiled=True,
    )
    other = lax.ppermute(own, "c", swap)
    units, low_width = gate_mat.shape[1], first.shape[1]
    tall = nz * piece + RANK
    keep, give, hidden, down_coef, flags = pl.pallas_call(
        functools.partial(expert_kernel, (nz, nx, ny, nc, ne)),
        out_shape=(
            jax.ShapeDtypeStruct((nxy, tall, slots), F32),
            jax.ShapeDtypeStruct((nxy, tall, slots), BF),
            jax.ShapeDtypeStruct((slots, units), BF),
            jax.ShapeDtypeStruct((slots, low_width), BF),
            jax.ShapeDtypeStruct((slots, low_width), F32),
        ),
        in_specs=[in_smem] + [in_vmem] * 8,
        out_specs=(in_vmem,) * 5,
        scratch_shapes=[pltpu.VMEM((features, slots), F32)],
        compiler_params=pltpu.CompilerParams(vmem_limit_bytes=40 << 20),
        cost_estimate=pl.CostEstimate(
            flops=10 * slots * features * units, bytes_accessed=9 << 20, transcendentals=slots * units
        ),
    )(
        me_c.reshape(1).astype(jnp.int32),
        own,
        other,
        held[:, 2 * width :],
        gate_mat,
        up_mat,
        down_mat,
        first,
        second,
    )
    grad_a = dot(hidden, down_coef, 0, 0)
    pair = (keep + lax.ppermute(give, "c", swap).astype(F32)).astype(BF)
    plane = lax.all_to_all(pair, ("x", "y"), split_axis=0, concat_axis=0, tiled=True)
    plane = jnp.sum(plane.astype(F32), axis=0)

    feats, low_own = plane[: nz * piece].reshape(nz, piece, slots), plane[nz * piece :]
    me_z = lax.axis_index("zh")

    def block(step):
        return lax.dynamic_index_in_dim(feats, (me_z + step) % nz, 0, keepdims=False)

    def pass_on(rows, low, step):
        sent = jnp.concatenate([rows, low], axis=0).astype(BF)
        got = lax.ppermute(sent, "zh", [(i, (i + step) % nz) for i in range(nz)]).astype(F32)
        return got[:piece], got[piece:]

    far_rows, low_below = pass_on(block(2), low_own, 1)
    rows_above, low_above = pass_on(block(nz - 1), low_own, nz - 1)
    rows_below, low_far = pass_on(block(1) + far_rows, low_below, 1)
    total = block(0) + rows_above + rows_below
    low_all = low_own + low_above + low_below + low_far

    lanes = 128
    feats = total.reshape(piece, ne, CAP).transpose(1, 0, 2)
    came = lax.all_to_all(
        feats.reshape(ne, piece * CAP // lanes, lanes),
        "e",
        split_axis=0,
        concat_axis=0,
        tiled=True,
    )
    returned = came.reshape(ne, piece, CAP).transpose(1, 0, 2).reshape(piece, slots)
    input_grad = dot(combine, returned, 0, 1, lax.Precision.HIGHEST).astype(BF)

    tiled = jnp.tile(low_all, (TEN, 1))
    up_coef = (SCALE * flags * tiled.T).astype(BF)
    local = lax.dynamic_index_in_dim(
        own.reshape(ny, nx * quarter_rows, 2 * width), me_y, 0, keepdims=False
    )[:, width:]
    grad_b = dot(up_coef, local, 0, 0)
    return input_grad, grad_a[None], grad_b[None]


def solution(mesh):
    tensor, dp, expert = mesh.shape["tensor"], mesh.shape["dp"], mesh.shape["expert"]
    fine = Mesh(
        mesh.devices.reshape(dp // 4, 4, expert, tensor // 2, 2), ("zh", "x", "e", "y", "c")
    )
    units, cols = ("zh", "x", "y", "c"), ("y", "c")
    return jax.shard_map(
        on_device,
        mesh=fine,
        in_specs=(
            P("e", cols),
            P("e", cols),
            P("e", None),
            P("e", None),
            P("e"),
            P("e", None, units),
            P("e", None, units),
            P("e", units, None),
            P("e", units, None),
            P("e", None, None),
        ),
        out_specs=(P("e", units), P("e", units, None), P("e", None, cols)),
        check_vma=False,
    )
```

```python
import functools

import jax
import jax.numpy as jnp
from jax import lax
from jax.experimental import pallas as pl
from jax.experimental.pallas import tpu as pltpu
from jax.sharding import Mesh, PartitionSpec as P

TEN = 8
RANK = 16
CAP = 32
SCALE = 2.0
BF = jnp.bfloat16
F32 = jnp.float32


def dot(a, b, ca, cb, precision=None):
    return lax.dot_general(
        a, b, (((ca,), (cb,)), ((), ())), precision=precision, preferred_element_type=F32
    )


def dispatch_kernel(nx, ne, where, ids, probs, tenants, tokens, cotangent, send, combine):
    group, width = tokens.shape
    part = CAP // nx
    shift = part.bit_length() - 1
    rank_in = functools.partial(lax.broadcasted_iota, jnp.int32)
    named = [rank_in((ne, group), 0) == ids[j : j + 1, :] for j in range(2)]
    either = (named[0] | named[1]).astype(F32).astype(BF)
    before = (rank_in((group, group), 0) < rank_in((group, group), 1)).astype(F32).astype(BF)
    earlier = dot(either, before, 1, 0)
    pick, marks, back = None, None, None
    for j in range(2):
        expert = ids[j : j + 1, :]
        slot = jnp.sum(jnp.where(named[j], earlier, 0.0), axis=0, keepdims=True).astype(jnp.int32)
        quarter, rest = slot >> shift, slot & (part - 1)
        here = rank_in((ne * part, group), 0) == expert * part + rest
        mine = jnp.where(here & (quarter == where[0]), 1.0, 0.0)
        weighted = jnp.where(here, probs[j : j + 1, :].astype(F32), 0.0).astype(BF)
        column = rank_in((128, group), 0) == quarter * TEN + tenants[...]
        mark = dot(weighted, jnp.where(column, 1.0, 0.0).astype(BF), 1, 1)
        home = jnp.where(rank_in((ne * CAP, group), 0) == expert * CAP + slot, 1.0, 0.0)
        pick = mine if pick is None else pick + mine
        marks = mark if marks is None else marks + mark
        back = home if back is None else back + home
    pick = pick.astype(BF)
    rows = [dot(pick, tokens[...], 1, 0), dot(pick, cotangent[...], 1, 0), marks]
    rows = jnp.concatenate(rows, 1).reshape(ne, part, 2 * width + 128)
    send[...] = rows.astype(BF)
    combine[...] = back


def expert_kernel(
    sizes, core, own, other, held_marks, ahead_mat, behind_mat, first,
    keep, give, hidden_out, down_out, flags_out, terms,
):
    nz, nx, ny, nc, ne = sizes
    nxy = nx * ny
    mine = core[0]
    quarter_rows, width = own.shape[1], own.shape[2] // 2
    slots = nx * quarter_rows
    features, units = ahead_mat.shape[0], ahead_mat.shape[1] // 2
    part, piece = features // nz, features // (nz * nxy * nc)
    low_width = first.shape[1]

    forward, backward = None, None
    for y in range(ny):
        for ref, at_core in ((own, mine), (other, 1 - mine)):
            at = pl.multiple_of((y * nc + at_core) * width, 128)
            both = ref[y * nx : (y + 1) * nx].reshape(slots, 2 * width)
            ahead = dot(both[:, :width], ahead_mat[pl.ds(at, width), :], 1, 0)
            behind = dot(both[:, width:], behind_mat[:, pl.ds(at, width)], 1, 1)
            forward = ahead if forward is None else forward + ahead
            backward = behind if backward is None else backward + behind
    gate_acc, up_acc = forward[:, :units], forward[:, units:]
    back_acc, low_back = backward[:, :units], backward[:, units:]

    mark_rows = held_marks[...]
    lane = lax.broadcasted_iota(jnp.int32, (mark_rows.shape[1], low_width), 0)
    tenant_of = lax.broadcasted_iota(jnp.int32, (mark_rows.shape[1], low_width), 1) // RANK
    flags, weight = [], []
    for x in range(nx):
        flags.append(dot(mark_rows, (lane == x * TEN + tenant_of).astype(BF), 1, 0))
        inside = (lane >= x * TEN) & (lane < (x + 1) * TEN)
        weight.append(dot(mark_rows, inside.astype(BF), 1, 0))
    flags, weight = jnp.concatenate(flags, 0), jnp.concatenate(weight, 0)[:, :1]

    sig = jax.nn.sigmoid(gate_acc)
    silu = gate_acc * sig
    hidden = (silu * up_acc).astype(BF)
    low_part = dot(hidden, first[...], 1, 0)
    down_coef = (SCALE * flags * low_back).astype(BF)
    hidden_grad = weight * back_acc + dot(down_coef, first[...], 1, 1)
    slope = sig * (1.0 + gate_acc * (1.0 - sig))
    gate_grad = hidden_grad * up_acc * slope
    up_grad = hidden_grad * silu
    hidden_out[...] = hidden
    down_out[...] = down_coef
    flags_out[...] = flags

    grads = jnp.concatenate([gate_grad, up_grad], 1)
    size = quarter_rows // ne
    starts = [x * quarter_rows + e * size for e in range(ne) for x in range(nx)]
    grads = jnp.concatenate([grads[at : at + size] for at in starts], 0).astype(BF)
    for z in range(nz):
        at = slice(z * part, (z + 1) * part)
        terms[at, :] = dot(ahead_mat[at, :], grads, 1, 1)

    rank_of = lax.broadcasted_iota(jnp.int32, (RANK, low_width), 1) % RANK
    fold = (rank_of == lax.broadcasted_iota(jnp.int32, (RANK, low_width), 0)).astype(BF)
    kept = jnp.where(flags != 0.0, low_part, 0.0).astype(BF)
    low_rows = dot(fold, kept, 1, 1)
    for p in range(nxy):
        for out, at_core in ((keep, mine), (give, 1 - mine)):
            chunks = [
                terms[pl.ds(pl.multiple_of(z * part + (p * nc + at_core) * piece, 8), piece), :]
                for z in range(nz)
            ]
            chunks.append(low_rows)
            out[p] = jnp.concatenate(chunks, 0).astype(out.dtype)


def on_device(
    tokens,
    cotangent,
    expert_ids,
    gate_probs,
    tenant_ids,
    w_gate,
    w_up,
    w_down,
    adapter_in,
    adapter_out,
):
    nz, nx, ne, ny, nc = (lax.axis_size(a) for a in ("zh", "x", "e", "y", "c"))
    nxy = nx * ny
    group, width = tokens.shape
    slots = ne * CAP
    part = CAP // nx
    me_x, me_y, me_c = (lax.axis_index(a) for a in ("x", "y", "c"))
    swap = [(0, 1), (1, 0)]
    gate_mat, up_mat, down_mat = w_gate[0], w_up[0], w_down[0]
    first, second = adapter_in[0], adapter_out[0]
    features = gate_mat.shape[0]
    piece = features // (nz * nxy * nc)

    in_vmem = pl.BlockSpec(memory_space=pltpu.VMEM)
    in_smem = pl.BlockSpec(memory_space=pltpu.SMEM)
    send, combine = pl.pallas_call(
        functools.partial(dispatch_kernel, nx, ne),
        out_shape=(
            jax.ShapeDtypeStruct((ne, part, 2 * width + 128), BF),
            jax.ShapeDtypeStruct((slots, group), F32),
        ),
        in_specs=[in_smem] + [in_vmem] * 5,
        out_specs=(in_vmem,) * 2,
    )(
        me_x.reshape(1).astype(jnp.int32),
        expert_ids.T,
        gate_probs.T,
        tenant_ids[None],
        tokens,
        cotangent,
    )
    held = lax.all_to_all(send, "e", split_axis=0, concat_axis=0, tiled=True)
    held = held.reshape(ne * part, -1)

    quarter_rows = ne * part
    block = held[:, : 2 * width]
    own = lax.all_to_all(
        jnp.broadcast_to(block[None], (nxy, quarter_rows, 2 * width)),
        ("y", "x"),
        split_axis=0,
        concat_axis=0,
        tiled=True,
    )
    own, *mats = lax.optimization_barrier((own, gate_mat, up_mat, down_mat, second))
    other = lax.ppermute(own, "c", swap)
    ahead_mat = jnp.concatenate(mats[:2], axis=1)
    behind_mat = jnp.concatenate(mats[2:], axis=0)
    units, low_width = gate_mat.shape[1], first.shape[1]
    tall = nz * piece + RANK
    keep, give, hidden, down_coef, flags = pl.pallas_call(
        functools.partial(expert_kernel, (nz, nx, ny, nc, ne)),
        out_shape=(
            jax.ShapeDtypeStruct((nxy, tall, slots), F32),
            jax.ShapeDtypeStruct((nxy, tall, slots), BF),
            jax.ShapeDtypeStruct((slots, units), BF),
            jax.ShapeDtypeStruct((slots, low_width), BF),
            jax.ShapeDtypeStruct((slots, low_width), F32),
        ),
        in_specs=[in_smem] + [in_vmem] * 6,
        out_specs=(in_vmem,) * 5,
        scratch_shapes=[pltpu.VMEM((features, slots), F32)],
        compiler_params=pltpu.CompilerParams(vmem_limit_bytes=40 << 20),
        cost_estimate=pl.CostEstimate(
            flops=10 * slots * features * units, bytes_accessed=9 << 20, transcendentals=slots * units
        ),
    )(
        me_c.reshape(1).astype(jnp.int32),
        own,
        other,
        held[:, 2 * width :],
        ahead_mat,
        behind_mat,
        first,
    )
    grad_a = dot(hidden, down_coef, 0, 0)
    pair = (keep + lax.ppermute(give, "c", swap).astype(F32)).astype(BF)
    plane = lax.all_to_all(pair, ("x", "y"), split_axis=0, concat_axis=0, tiled=True)
    plane = jnp.sum(plane.astype(F32), axis=0)

    feats, low_own = plane[: nz * piece].reshape(nz, piece, slots), plane[nz * piece :]
    me_z = lax.axis_index("zh")

    def block(step):
        return lax.dynamic_index_in_dim(feats, (me_z + step) % nz, 0, keepdims=False)

    def pass_on(rows, low, step):
        sent = jnp.concatenate([rows, low], axis=0).astype(BF)
        got = lax.ppermute(sent, "zh", [(i, (i + step) % nz) for i in range(nz)]).astype(F32)
        return got[:piece], got[piece:]

    far_rows, low_below = pass_on(block(2), low_own, 1)
    rows_above, low_above = pass_on(block(nz - 1), low_own, nz - 1)
    rows_below, low_far = pass_on(block(1) + far_rows, low_below, 1)
    total = block(0) + rows_above + rows_below
    low_all = low_own + low_above + low_below + low_far

    lanes = 128
    feats = total.reshape(piece, ne, CAP).transpose(1, 0, 2)
    came = lax.all_to_all(
        feats.reshape(ne, piece * CAP // lanes, lanes),
        "e",
        split_axis=0,
        concat_axis=0,
        tiled=True,
    )
    returned = came.reshape(ne, piece, CAP).transpose(1, 0, 2).reshape(piece, slots)
    input_grad = dot(combine, returned, 0, 1, lax.Precision.HIGHEST).astype(BF)

    tiled = jnp.tile(low_all, (TEN, 1))
    up_coef = (SCALE * flags * tiled.T).astype(BF)
    local = lax.dynamic_index_in_dim(
        own.reshape(ny, nx * quarter_rows, 2 * width), me_y, 0, keepdims=False
    )[:, width:]
    grad_b = dot(up_coef, local, 0, 0)
    return input_grad, grad_a[None], grad_b[None]


def solution(mesh):
    tensor, dp, expert = mesh.shape["tensor"], mesh.shape["dp"], mesh.shape["expert"]
    fine = Mesh(
        mesh.devices.reshape(dp // 4, 4, expert, tensor // 2, 2), ("zh", "x", "e", "y", "c")
    )
    units, cols = ("zh", "x", "y", "c"), ("y", "c")
    return jax.shard_map(
        on_device,
        mesh=fine,
        in_specs=(
            P("e", cols),
            P("e", cols),
            P("e", None),
            P("e", None),
            P("e"),
            P("e", None, units),
            P("e", None, units),
            P("e", units, None),
            P("e", units, None),
            P("e", None, None),
        ),
        out_specs=(P("e", units), P("e", units, None), P("e", None, cols)),
        check_vma=False,
    )
```

```python
import functools

import jax
import jax.numpy as jnp
from jax import lax
from jax.experimental import pallas as pl
from jax.experimental.pallas import tpu as pltpu
from jax.sharding import Mesh, PartitionSpec as P

TEN = 8
RANK = 16
CAP = 32
SCALE = 2.0
BF = jnp.bfloat16
F32 = jnp.float32


def dot(a, b, ca, cb, precision=None):
    return lax.dot_general(
        a, b, (((ca,), (cb,)), ((), ())), precision=precision, preferred_element_type=F32
    )


def dispatch_kernel(nx, ne, where, ids, probs, tenants, tokens, cotangent, send, combine):
    group, width = tokens.shape
    part = CAP // nx
    shift = part.bit_length() - 1
    rank_in = functools.partial(lax.broadcasted_iota, jnp.int32)
    named = [rank_in((ne, group), 0) == ids[j : j + 1, :] for j in range(2)]
    either = (named[0] | named[1]).astype(F32).astype(BF)
    before = (rank_in((group, group), 0) < rank_in((group, group), 1)).astype(F32).astype(BF)
    earlier = dot(either, before, 1, 0)
    pick, marks, back = None, None, None
    for j in range(2):
        expert = ids[j : j + 1, :]
        slot = jnp.sum(jnp.where(named[j], earlier, 0.0), axis=0, keepdims=True).astype(jnp.int32)
        quarter, rest = slot >> shift, slot & (part - 1)
        here = rank_in((ne * part, group), 0) == expert * part + rest
        mine = jnp.where(here & (quarter == where[0]), 1.0, 0.0)
        weighted = jnp.where(here, probs[j : j + 1, :].astype(F32), 0.0).astype(BF)
        column = rank_in((128, group), 0) == quarter * TEN + tenants[...]
        mark = dot(weighted, jnp.where(column, 1.0, 0.0).astype(BF), 1, 1)
        home = jnp.where(rank_in((ne * CAP, group), 0) == expert * CAP + slot, 1.0, 0.0)
        pick = mine if pick is None else pick + mine
        marks = mark if marks is None else marks + mark
        back = home if back is None else back + home
    pick = pick.astype(BF)
    rows = [dot(pick, tokens[...], 1, 0), dot(pick, cotangent[...], 1, 0), marks]
    rows = jnp.concatenate(rows, 1).reshape(ne, part, 2 * width + 128)
    send[...] = rows.astype(BF)
    combine[...] = back


def expert_kernel(
    sizes, core, own, other, held_marks, ahead_mat, behind_mat, first,
    keep, give, hidden_out, down_out, flags_out, terms,
):
    nz, nx, ny, nc, ne = sizes
    nxy = nx * ny
    mine = core[0]
    quarter_rows, width = own.shape[1], own.shape[2] // 2
    slots = nx * quarter_rows
    features, units = ahead_mat.shape[0], ahead_mat.shape[1] // 2
    part, piece = features // nz, features // (nz * nxy * nc)
    low_width = first.shape[1]

    forward, backward = None, None
    for y in range(ny):
        for ref, at_core in ((own, mine), (other, 1 - mine)):
            at = pl.multiple_of((y * nc + at_core) * width, 128)
            both = ref[y * nx : (y + 1) * nx].reshape(slots, 2 * width)
            ahead = dot(both[:, :width], ahead_mat[pl.ds(at, width), :], 1, 0)
            behind = dot(both[:, width:], behind_mat[:, pl.ds(at, width)], 1, 1)
            forward = ahead if forward is None else forward + ahead
            backward = behind if backward is None else backward + behind
    gate_acc, up_acc = forward[:, :units], forward[:, units:]
    back_acc, low_back = backward[:, :units], backward[:, units:]

    mark_rows = held_marks[...]
    lane = lax.broadcasted_iota(jnp.int32, (mark_rows.shape[1], low_width), 0)
    tenant_of = lax.broadcasted_iota(jnp.int32, (mark_rows.shape[1], low_width), 1) // RANK
    flags, weight = [], []
    for x in range(nx):
        flags.append(dot(mark_rows, (lane == x * TEN + tenant_of).astype(BF), 1, 0))
        inside = (lane >= x * TEN) & (lane < (x + 1) * TEN)
        weight.append(dot(mark_rows, inside.astype(BF), 1, 0))
    flags, weight = jnp.concatenate(flags, 0), jnp.concatenate(weight, 0)[:, :1]

    sig = jax.nn.sigmoid(gate_acc)
    silu = gate_acc * sig
    hidden = (silu * up_acc).astype(BF)
    low_part = dot(hidden, first[...], 1, 0)
    down_coef = (SCALE * flags * low_back).astype(BF)
    hidden_grad = weight * back_acc + dot(down_coef, first[...], 1, 1)
    slope = sig * (1.0 + gate_acc * (1.0 - sig))
    gate_grad = hidden_grad * up_acc * slope
    up_grad = hidden_grad * silu
    hidden_out[...] = hidden
    down_out[...] = down_coef
    flags_out[...] = flags

    grads = jnp.concatenate([gate_grad, up_grad], 1)
    size = quarter_rows // ne
    starts = [x * quarter_rows + e * size for e in range(ne) for x in range(nx)]
    grads = jnp.concatenate([grads[at : at + size] for at in starts], 0).astype(BF)
    for z in range(nz):
        at = slice(z * part, (z + 1) * part)
        terms[at, :] = dot(ahead_mat[at, :], grads, 1, 1)

    rank_of = lax.broadcasted_iota(jnp.int32, (RANK, low_width), 1) % RANK
    fold = (rank_of == lax.broadcasted_iota(jnp.int32, (RANK, low_width), 0)).astype(BF)
    kept = jnp.where(flags != 0.0, low_part, 0.0).astype(BF)
    low_rows = dot(fold, kept, 1, 1)
    for p in range(nxy):
        for out, at_core in ((keep, mine), (give, 1 - mine)):
            chunks = [
                terms[pl.ds(pl.multiple_of(z * part + (p * nc + at_core) * piece, 8), piece), :]
                for z in range(nz)
            ]
            chunks.append(low_rows)
            out[p] = jnp.concatenate(chunks, 0).astype(out.dtype)


def on_device(
    tokens,
    cotangent,
    expert_ids,
    gate_probs,
    tenant_ids,
    w_gate,
    w_up,
    w_down,
    adapter_in,
    adapter_out,
):
    nz, nx, ne, ny, nc = (lax.axis_size(a) for a in ("zh", "x", "e", "y", "c"))
    nxy = nx * ny
    group, width = tokens.shape
    slots = ne * CAP
    part = CAP // nx
    me_x, me_y, me_c = (lax.axis_index(a) for a in ("x", "y", "c"))
    swap = [(0, 1), (1, 0)]
    gate_mat, up_mat, down_mat = w_gate[0], w_up[0], w_down[0]
    first, second = adapter_in[0], adapter_out[0]
    features = gate_mat.shape[0]
    piece = features // (nz * nxy * nc)

    in_vmem = pl.BlockSpec(memory_space=pltpu.VMEM)
    in_smem = pl.BlockSpec(memory_space=pltpu.SMEM)
    send, combine = pl.pallas_call(
        functools.partial(dispatch_kernel, nx, ne),
        out_shape=(
            jax.ShapeDtypeStruct((ne, part, 2 * width + 128), BF),
            jax.ShapeDtypeStruct((slots, group), F32),
        ),
        in_specs=[in_smem] + [in_vmem] * 5,
        out_specs=(in_vmem,) * 2,
    )(
        me_x.reshape(1).astype(jnp.int32),
        expert_ids.T,
        gate_probs.T,
        tenant_ids[None],
        tokens,
        cotangent,
    )
    held = lax.all_to_all(send, "e", split_axis=0, concat_axis=0, tiled=True)
    held = held.reshape(ne * part, -1)

    quarter_rows = ne * part
    block = held[:, : 2 * width]
    own = lax.all_to_all(
        jnp.broadcast_to(block[None], (nxy, quarter_rows, 2 * width)),
        ("y", "x"),
        split_axis=0,
        concat_axis=0,
        tiled=True,
    )
    own, *mats = lax.optimization_barrier((own, gate_mat, up_mat, down_mat, second))
    other = lax.ppermute(own, "c", swap)
    ahead_mat = jnp.concatenate(mats[:2], axis=1)
    behind_mat = jnp.concatenate(mats[2:], axis=0)
    units, low_width = gate_mat.shape[1], first.shape[1]
    tall = nz * piece + RANK
    keep, give, hidden, down_coef, flags = pl.pallas_call(
        functools.partial(expert_kernel, (nz, nx, ny, nc, ne)),
        out_shape=(
            jax.ShapeDtypeStruct((nxy, tall, slots), F32),
            jax.ShapeDtypeStruct((nxy, tall, slots), BF),
            jax.ShapeDtypeStruct((slots, units), BF),
            jax.ShapeDtypeStruct((slots, low_width), BF),
            jax.ShapeDtypeStruct((slots, low_width), F32),
        ),
        in_specs=[in_smem] + [in_vmem] * 6,
        out_specs=(in_vmem,) * 5,
        scratch_shapes=[pltpu.VMEM((features, slots), F32)],
        compiler_params=pltpu.CompilerParams(vmem_limit_bytes=40 << 20),
        cost_estimate=pl.CostEstimate(
            flops=10 * slots * features * units, bytes_accessed=9 << 20, transcendentals=slots * units
        ),
    )(
        me_c.reshape(1).astype(jnp.int32),
        own,
        other,
        held[:, 2 * width :],
        ahead_mat,
        behind_mat,
        first,
    )
    grad_a = dot(hidden, down_coef, 0, 0)
    pair = (keep + lax.ppermute(give, "c", swap).astype(F32)).astype(BF)
    plane = lax.all_to_all(pair, ("x", "y"), split_axis=0, concat_axis=0, tiled=True)
    plane = jnp.sum(plane.astype(F32), axis=0)

    blocks, low_own = plane[: nz * piece].reshape(nz, piece, slots), plane[nz * piece :]
    me_z = lax.axis_index("zh")

    def block(mask):
        return lax.dynamic_index_in_dim(blocks, me_z ^ mask, 0, keepdims=False)

    def swapped(parts, mask):
        sent = jnp.concatenate(parts, axis=0).astype(BF)
        return lax.ppermute(sent, "zh", [(i, i ^ mask) for i in range(nz)]).astype(F32)

    got = swapped([block(1), block(2), low_own], 1)
    pair_own, pair_far = block(0) + got[:piece], block(3) + got[piece : 2 * piece]
    pair_low = low_own + got[2 * piece :]
    got = swapped([pair_far, pair_low], 3)
    total, low_all = pair_own + got[:piece], pair_low + got[piece:]

    lanes = 128
    feats = total.reshape(piece, ne, CAP).transpose(1, 0, 2)
    came = lax.all_to_all(
        feats.reshape(ne, piece * CAP // lanes, lanes),
        "e",
        split_axis=0,
        concat_axis=0,
        tiled=True,
    )
    returned = came.reshape(ne, piece, CAP).transpose(1, 0, 2).reshape(piece, slots)
    input_grad = dot(combine, returned, 0, 1, lax.Precision.HIGHEST).astype(BF)

    tiled = jnp.tile(low_all, (TEN, 1))
    up_coef = (SCALE * flags * tiled.T).astype(BF)
    local = lax.dynamic_index_in_dim(
        own.reshape(ny, nx * quarter_rows, 2 * width), me_y, 0, keepdims=False
    )[:, width:]
    grad_b = dot(up_coef, local, 0, 0)
    return input_grad, grad_a[None], grad_b[None]


def solution(mesh):
    tensor, dp, expert = mesh.shape["tensor"], mesh.shape["dp"], mesh.shape["expert"]
    fine = Mesh(
        mesh.devices.reshape(dp // 4, 4, expert, tensor // 2, 2), ("zh", "x", "e", "y", "c")
    )
    units, cols = ("zh", "x", "y", "c"), ("y", "c")
    return jax.shard_map(
        on_device,
        mesh=fine,
        in_specs=(
            P("e", cols),
            P("e", cols),
            P("e", None),
            P("e", None),
            P("e"),
            P("e", None, units),
            P("e", None, units),
            P("e", units, None),
            P("e", units, None),
            P("e", None, None),
        ),
        out_specs=(P("e", units), P("e", units, None), P("e", None, cols)),
        check_vma=False,
    )
```

```python
import functools

import jax
import jax.numpy as jnp
from jax import lax
from jax.experimental import pallas as pl
from jax.experimental.pallas import tpu as pltpu
from jax.sharding import Mesh, PartitionSpec as P

TEN = 8
RANK = 16
CAP = 32
SCALE = 2.0
BF = jnp.bfloat16
F32 = jnp.float32


def dot(a, b, ca, cb, precision=None):
    return lax.dot_general(
        a, b, (((ca,), (cb,)), ((), ())), precision=precision, preferred_element_type=F32
    )


def dispatch_kernel(nx, ne, where, ids, probs, tenants, tokens, cotangent, send, combine):
    group, width = tokens.shape
    part = CAP // nx
    shift = part.bit_length() - 1
    rank_in = functools.partial(lax.broadcasted_iota, jnp.int32)
    named = [rank_in((ne, group), 0) == ids[j : j + 1, :] for j in range(2)]
    either = (named[0] | named[1]).astype(F32).astype(BF)
    before = (rank_in((group, group), 0) < rank_in((group, group), 1)).astype(F32).astype(BF)
    earlier = dot(either, before, 1, 0)
    pick, marks, back = None, None, None
    for j in range(2):
        expert = ids[j : j + 1, :]
        slot = jnp.sum(jnp.where(named[j], earlier, 0.0), axis=0, keepdims=True).astype(jnp.int32)
        quarter, rest = slot >> shift, slot & (part - 1)
        here = rank_in((ne * part, group), 0) == expert * part + rest
        mine = jnp.where(here & (quarter == where[0]), 1.0, 0.0)
        weighted = jnp.where(here, probs[j : j + 1, :].astype(F32), 0.0).astype(BF)
        column = rank_in((128, group), 0) == quarter * TEN + tenants[...]
        mark = dot(weighted, jnp.where(column, 1.0, 0.0).astype(BF), 1, 1)
        home = jnp.where(rank_in((ne * CAP, group), 0) == expert * CAP + slot, 1.0, 0.0)
        pick = mine if pick is None else pick + mine
        marks = mark if marks is None else marks + mark
        back = home if back is None else back + home
    pick = pick.astype(BF)
    rows = [dot(pick, tokens[...], 1, 0), dot(pick, cotangent[...], 1, 0), marks]
    rows = jnp.concatenate(rows, 1).reshape(ne, part, 2 * width + 128)
    send[...] = rows.astype(BF)
    combine[...] = back


def expert_kernel(
    sizes, core, own, other, held_marks, ahead_mat, behind_mat, first,
    keep, give, hidden_out, down_out, flags_out, terms,
):
    nz, nx, ny, nc, ne = sizes
    nxy = nx * ny
    mine = core[0]
    quarter_rows, width = own.shape[1], own.shape[2] // 2
    slots = nx * quarter_rows
    features, units = ahead_mat.shape[0], ahead_mat.shape[1] // 2
    part, piece = features // nz, features // (nz * nxy * nc)
    low_width = first.shape[1]

    forward, backward = None, None
    for y in range(ny):
        for ref, at_core in ((own, mine), (other, 1 - mine)):
            at = pl.multiple_of((y * nc + at_core) * width, 128)
            both = ref[y * nx : (y + 1) * nx].reshape(slots, 2 * width)
            ahead = dot(both[:, :width], ahead_mat[pl.ds(at, width), :], 1, 0)
            behind = dot(both[:, width:], behind_mat[:, pl.ds(at, width)], 1, 1)
            forward = ahead if forward is None else forward + ahead
            backward = behind if backward is None else backward + behind
    gate_acc, up_acc = forward[:, :units], forward[:, units:]
    back_acc, low_back = backward[:, :units], backward[:, units:]

    mark_rows = held_marks[...]
    lane = lax.broadcasted_iota(jnp.int32, (mark_rows.shape[1], low_width), 0)
    tenant_of = lax.broadcasted_iota(jnp.int32, (mark_rows.shape[1], low_width), 1) // RANK
    flags, weight = [], []
    for x in range(nx):
        flags.append(dot(mark_rows, (lane == x * TEN + tenant_of).astype(BF), 1, 0))
        inside = (lane >= x * TEN) & (lane < (x + 1) * TEN)
        weight.append(dot(mark_rows, inside.astype(BF), 1, 0))
    flags, weight = jnp.concatenate(flags, 0), jnp.concatenate(weight, 0)[:, :1]

    sig = jax.nn.sigmoid(gate_acc)
    silu = gate_acc * sig
    hidden = (silu * up_acc).astype(BF)
    low_part = dot(hidden, first[...], 1, 0)
    down_coef = (SCALE * flags * low_back).astype(BF)
    hidden_grad = weight * back_acc + dot(down_coef, first[...], 1, 1)
    slope = sig * (1.0 + gate_acc * (1.0 - sig))
    gate_grad = hidden_grad * up_acc * slope
    up_grad = hidden_grad * silu
    hidden_out[...] = hidden
    down_out[...] = down_coef
    flags_out[...] = flags

    grads = jnp.concatenate([gate_grad, up_grad], 1)
    size = quarter_rows // ne
    starts = [x * quarter_rows + e * size for e in range(ne) for x in range(nx)]
    grads = jnp.concatenate([grads[at : at + size] for at in starts], 0).astype(BF)
    for z in range(nz):
        at = slice(z * part, (z + 1) * part)
        terms[at, :] = dot(ahead_mat[at, :], grads, 1, 1)

    rank_of = lax.broadcasted_iota(jnp.int32, (RANK, low_width), 1) % RANK
    fold = (rank_of == lax.broadcasted_iota(jnp.int32, (RANK, low_width), 0)).astype(BF)
    kept = jnp.where(flags != 0.0, low_part, 0.0).astype(BF)
    low_rows = dot(fold, kept, 1, 1)
    for p in range(nxy):
        for out, at_core in ((keep, mine), (give, 1 - mine)):
            chunks = [
                terms[pl.ds(pl.multiple_of(z * part + (p * nc + at_core) * piece, 8), piece), :]
                for z in range(nz)
            ]
            chunks.append(low_rows)
            out[p] = jnp.concatenate(chunks, 0).astype(out.dtype)


def on_device(
    tokens,
    cotangent,
    expert_ids,
    gate_probs,
    tenant_ids,
    w_gate,
    w_up,
    w_down,
    adapter_in,
    adapter_out,
):
    nz, nx, ne, ny, nc = (lax.axis_size(a) for a in ("zh", "x", "e", "y", "c"))
    nxy = nx * ny
    group, width = tokens.shape
    slots = ne * CAP
    part = CAP // nx
    me_x, me_y, me_c = (lax.axis_index(a) for a in ("x", "y", "c"))
    swap = [(0, 1), (1, 0)]
    gate_mat, up_mat, down_mat = w_gate[0], w_up[0], w_down[0]
    first, second = adapter_in[0], adapter_out[0]
    features = gate_mat.shape[0]
    piece = features // (nz * nxy * nc)

    in_vmem = pl.BlockSpec(memory_space=pltpu.VMEM)
    in_smem = pl.BlockSpec(memory_space=pltpu.SMEM)
    send, combine = pl.pallas_call(
        functools.partial(dispatch_kernel, nx, ne),
        out_shape=(
            jax.ShapeDtypeStruct((ne, part, 2 * width + 128), BF),
            jax.ShapeDtypeStruct((slots, group), F32),
        ),
        in_specs=[in_smem] + [in_vmem] * 5,
        out_specs=(in_vmem,) * 2,
    )(
        me_x.reshape(1).astype(jnp.int32),
        expert_ids.T,
        gate_probs.T,
        tenant_ids[None],
        tokens,
        cotangent,
    )
    held = lax.all_to_all(send, "e", split_axis=0, concat_axis=0, tiled=True)
    held = held.reshape(ne * part, -1)

    quarter_rows = ne * part
    block = held[:, : 2 * width]
    own = lax.all_to_all(
        jnp.broadcast_to(block[None], (nxy, quarter_rows, 2 * width)),
        ("y", "x"),
        split_axis=0,
        concat_axis=0,
        tiled=True,
    )
    own, *mats = lax.optimization_barrier((own, gate_mat, up_mat, down_mat, second))
    other = lax.ppermute(own, "c", swap)
    ahead_mat = jnp.concatenate(mats[:2], axis=1)
    behind_mat = jnp.concatenate(mats[2:], axis=0)
    units, low_width = gate_mat.shape[1], first.shape[1]
    tall = nz * piece + RANK
    keep, give, hidden, down_coef, flags = pl.pallas_call(
        functools.partial(expert_kernel, (nz, nx, ny, nc, ne)),
        out_shape=(
            jax.ShapeDtypeStruct((nxy, tall, slots), F32),
            jax.ShapeDtypeStruct((nxy, tall, slots), BF),
            jax.ShapeDtypeStruct((slots, units), BF),
            jax.ShapeDtypeStruct((slots, low_width), BF),
            jax.ShapeDtypeStruct((slots, low_width), F32),
        ),
        in_specs=[in_smem] + [in_vmem] * 6,
        out_specs=(in_vmem,) * 5,
        scratch_shapes=[pltpu.VMEM((features, slots), F32)],
        compiler_params=pltpu.CompilerParams(vmem_limit_bytes=40 << 20),
        cost_estimate=pl.CostEstimate(
            flops=10 * slots * features * units, bytes_accessed=9 << 20, transcendentals=slots * units
        ),
    )(
        me_c.reshape(1).astype(jnp.int32),
        own,
        other,
        held[:, 2 * width :],
        ahead_mat,
        behind_mat,
        first,
    )
    pair = (keep + lax.ppermute(give, "c", swap).astype(F32)).astype(BF)
    plane = lax.all_to_all(pair, ("x", "y"), split_axis=0, concat_axis=0, tiled=True)
    plane, hidden, down_coef, flags, own, combine = lax.optimization_barrier(
        (plane, hidden, down_coef, flags, own, combine)
    )
    plane = jnp.sum(plane.astype(F32), axis=0)
    grad_a = dot(hidden, down_coef, 0, 0)

    feats, low_own = plane[: nz * piece].reshape(nz, piece, slots), plane[nz * piece :]
    me_z = lax.axis_index("zh")

    def block(step):
        return lax.dynamic_index_in_dim(feats, (me_z + step) % nz, 0, keepdims=False)

    def pass_on(rows, low, step):
        sent = jnp.concatenate([rows, low], axis=0).astype(BF)
        got = lax.ppermute(sent, "zh", [(i, (i + step) % nz) for i in range(nz)]).astype(F32)
        return got[:piece], got[piece:]

    far_rows, low_below = pass_on(block(2), low_own, 1)
    rows_above, low_above = pass_on(block(nz - 1), low_own, nz - 1)
    rows_below, low_far = pass_on(block(1) + far_rows, low_below, 1)
    total = block(0) + rows_above + rows_below
    low_all = low_own + low_above + low_below + low_far

    lanes = 128
    feats = total.reshape(piece, ne, CAP).transpose(1, 0, 2)
    came = lax.all_to_all(
        feats.reshape(ne, piece * CAP // lanes, lanes),
        "e",
        split_axis=0,
        concat_axis=0,
        tiled=True,
    )
    returned = came.reshape(ne, piece, CAP).transpose(1, 0, 2).reshape(piece, slots)
    input_grad = dot(combine, returned, 0, 1, lax.Precision.HIGHEST).astype(BF)

    tiled = jnp.tile(low_all, (TEN, 1))
    up_coef = (SCALE * flags * tiled.T).astype(BF)
    local = lax.dynamic_index_in_dim(
        own.reshape(ny, nx * quarter_rows, 2 * width), me_y, 0, keepdims=False
    )[:, width:]
    grad_b = dot(up_coef, local, 0, 0)
    return input_grad, grad_a[None], grad_b[None]


def solution(mesh):
    tensor, dp, expert = mesh.shape["tensor"], mesh.shape["dp"], mesh.shape["expert"]
    fine = Mesh(
        mesh.devices.reshape(dp // 4, 4, expert, tensor // 2, 2), ("zh", "x", "e", "y", "c")
    )
    units, cols = ("zh", "x", "y", "c"), ("y", "c")
    return jax.shard_map(
        on_device,
        mesh=fine,
        in_specs=(
            P("e", cols),
            P("e", cols),
            P("e", None),
            P("e", None),
            P("e"),
            P("e", None, units),
            P("e", None, units),
            P("e", units, None),
            P("e", units, None),
            P("e", None, None),
        ),
        out_specs=(P("e", units), P("e", units, None), P("e", None, cols)),
        check_vma=False,
    )
```

```python
import functools

import jax
import jax.numpy as jnp
from jax import lax
from jax.experimental import pallas as pl
from jax.experimental.pallas import tpu as pltpu
from jax.sharding import Mesh, PartitionSpec as P

TEN = 8
RANK = 16
CAP = 32
SCALE = 2.0
BF = jnp.bfloat16
F32 = jnp.float32


def dot(a, b, ca, cb, precision=None):
    return lax.dot_general(
        a, b, (((ca,), (cb,)), ((), ())), precision=precision, preferred_element_type=F32
    )


def dispatch_kernel(nx, ne, where, ids, probs, tenants, tokens, cotangent, send, combine):
    group, width = tokens.shape
    part = CAP // nx
    shift = part.bit_length() - 1
    rank_in = functools.partial(lax.broadcasted_iota, jnp.int32)
    named = [rank_in((ne, group), 0) == ids[j : j + 1, :] for j in range(2)]
    either = (named[0] | named[1]).astype(F32).astype(BF)
    before = (rank_in((group, group), 0) < rank_in((group, group), 1)).astype(F32).astype(BF)
    earlier = dot(either, before, 1, 0)
    pick, marks, back = None, None, None
    for j in range(2):
        expert = ids[j : j + 1, :]
        slot = jnp.sum(jnp.where(named[j], earlier, 0.0), axis=0, keepdims=True).astype(jnp.int32)
        quarter, rest = slot >> shift, slot & (part - 1)
        here = rank_in((ne * part, group), 0) == expert * part + rest
        mine = jnp.where(here & (quarter == where[0]), 1.0, 0.0)
        weighted = jnp.where(here, probs[j : j + 1, :].astype(F32), 0.0).astype(BF)
        column = rank_in((128, group), 0) == quarter * TEN + tenants[...]
        mark = dot(weighted, jnp.where(column, 1.0, 0.0).astype(BF), 1, 1)
        home = jnp.where(rank_in((ne * CAP, group), 0) == expert * CAP + slot, 1.0, 0.0)
        pick = mine if pick is None else pick + mine
        marks = mark if marks is None else marks + mark
        back = home if back is None else back + home
    pick = pick.astype(BF)
    rows = [dot(pick, tokens[...], 1, 0), dot(pick, cotangent[...], 1, 0), marks]
    rows = jnp.concatenate(rows, 1).reshape(ne, part, 2 * width + 128)
    send[...] = rows.astype(BF)
    combine[...] = back


def expert_kernel(
    sizes, core, own, other, held_marks, ahead_mat, behind_mat, first,
    keep, give, hidden_out, down_out, flags_out, terms,
):
    nz, nx, ny, nc, ne = sizes
    nxy = nx * ny
    mine = core[0]
    quarter_rows, width = own.shape[1], own.shape[2] // 2
    slots = nx * quarter_rows
    features, units = ahead_mat.shape[0], ahead_mat.shape[1] // 2
    part, piece = features // nz, features // (nz * nxy * nc)
    low_width = first.shape[1]

    forward, backward = None, None
    for y in range(ny):
        for ref, at_core in ((own, mine), (other, 1 - mine)):
            at = pl.multiple_of((y * nc + at_core) * width, 128)
            both = ref[y * nx : (y + 1) * nx].reshape(slots, 2 * width)
            ahead = dot(both[:, :width], ahead_mat[pl.ds(at, width), :], 1, 0)
            behind = dot(both[:, width:], behind_mat[:, pl.ds(at, width)], 1, 1)
            forward = ahead if forward is None else forward + ahead
            backward = behind if backward is None else backward + behind
    gate_acc, up_acc = forward[:, :units], forward[:, units:]
    back_acc, low_back = backward[:, :units], backward[:, units:]

    mark_rows = held_marks[...]
    lane = lax.broadcasted_iota(jnp.int32, (mark_rows.shape[1], low_width), 0)
    tenant_of = lax.broadcasted_iota(jnp.int32, (mark_rows.shape[1], low_width), 1) // RANK
    flags, weight = [], []
    for x in range(nx):
        flags.append(dot(mark_rows, (lane == x * TEN + tenant_of).astype(BF), 1, 0))
        inside = (lane >= x * TEN) & (lane < (x + 1) * TEN)
        weight.append(dot(mark_rows, inside.astype(BF), 1, 0))
    flags, weight = jnp.concatenate(flags, 0), jnp.concatenate(weight, 0)[:, :1]

    sig = jax.nn.sigmoid(gate_acc)
    silu = gate_acc * sig
    hidden = (silu * up_acc).astype(BF)
    low_part = dot(hidden, first[...], 1, 0)
    down_coef = (SCALE * flags * low_back).astype(BF)
    hidden_grad = weight * back_acc + dot(down_coef, first[...], 1, 1)
    slope = sig * (1.0 + gate_acc * (1.0 - sig))
    gate_grad = hidden_grad * up_acc * slope
    up_grad = hidden_grad * silu
    hidden_out[...] = hidden
    down_out[...] = down_coef
    flags_out[...] = flags

    grads = jnp.concatenate([gate_grad, up_grad], 1)
    size = quarter_rows // ne
    starts = [x * quarter_rows + e * size for e in range(ne) for x in range(nx)]
    grads = jnp.concatenate([grads[at : at + size] for at in starts], 0).astype(BF)
    for z in range(nz):
        at = slice(z * part, (z + 1) * part)
        terms[at, :] = dot(ahead_mat[at, :], grads, 1, 1)

    rank_of = lax.broadcasted_iota(jnp.int32, (RANK, low_width), 1) % RANK
    fold = (rank_of == lax.broadcasted_iota(jnp.int32, (RANK, low_width), 0)).astype(BF)
    kept = jnp.where(flags != 0.0, low_part, 0.0).astype(BF)
    low_rows = dot(fold, kept, 1, 1)
    for p in range(nxy):
        for out, at_core in ((keep, mine), (give, 1 - mine)):
            chunks = [
                terms[pl.ds(pl.multiple_of(z * part + (p * nc + at_core) * piece, 8), piece), :]
                for z in range(nz)
            ]
            chunks.append(low_rows)
            out[p] = jnp.concatenate(chunks, 0).astype(out.dtype)


def add_kernel(kept, came, pair):
    for p in range(kept.shape[0]):
        pair[p] = (kept[p] + came[p].astype(F32)).astype(BF)


def on_device(
    tokens,
    cotangent,
    expert_ids,
    gate_probs,
    tenant_ids,
    w_gate,
    w_up,
    w_down,
    adapter_in,
    adapter_out,
):
    nz, nx, ne, ny, nc = (lax.axis_size(a) for a in ("zh", "x", "e", "y", "c"))
    nxy = nx * ny
    group, width = tokens.shape
    slots = ne * CAP
    part = CAP // nx
    me_x, me_y, me_c = (lax.axis_index(a) for a in ("x", "y", "c"))
    swap = [(0, 1), (1, 0)]
    gate_mat, up_mat, down_mat = w_gate[0], w_up[0], w_down[0]
    first, second = adapter_in[0], adapter_out[0]
    features = gate_mat.shape[0]
    piece = features // (nz * nxy * nc)

    in_vmem = pl.BlockSpec(memory_space=pltpu.VMEM)
    in_smem = pl.BlockSpec(memory_space=pltpu.SMEM)
    send, combine = pl.pallas_call(
        functools.partial(dispatch_kernel, nx, ne),
        out_shape=(
            jax.ShapeDtypeStruct((ne, part, 2 * width + 128), BF),
            jax.ShapeDtypeStruct((slots, group), F32),
        ),
        in_specs=[in_smem] + [in_vmem] * 5,
        out_specs=(in_vmem,) * 2,
    )(
        me_x.reshape(1).astype(jnp.int32),
        expert_ids.T,
        gate_probs.T,
        tenant_ids[None],
        tokens,
        cotangent,
    )
    held = lax.all_to_all(send, "e", split_axis=0, concat_axis=0, tiled=True)
    held = held.reshape(ne * part, -1)

    quarter_rows = ne * part
    block = held[:, : 2 * width]
    own = lax.all_to_all(
        jnp.broadcast_to(block[None], (nxy, quarter_rows, 2 * width)),
        ("y", "x"),
        split_axis=0,
        concat_axis=0,
        tiled=True,
    )
    own, *mats = lax.optimization_barrier((own, gate_mat, up_mat, down_mat, second))
    other = lax.ppermute(own, "c", swap)
    ahead_mat = jnp.concatenate(mats[:2], axis=1)
    behind_mat = jnp.concatenate(mats[2:], axis=0)
    units, low_width = gate_mat.shape[1], first.shape[1]
    tall = nz * piece + RANK
    keep, give, hidden, down_coef, flags = pl.pallas_call(
        functools.partial(expert_kernel, (nz, nx, ny, nc, ne)),
        out_shape=(
            jax.ShapeDtypeStruct((nxy, tall, slots), F32),
            jax.ShapeDtypeStruct((nxy, tall, slots), BF),
            jax.ShapeDtypeStruct((slots, units), BF),
            jax.ShapeDtypeStruct((slots, low_width), BF),
            jax.ShapeDtypeStruct((slots, low_width), F32),
        ),
        in_specs=[in_smem] + [in_vmem] * 6,
        out_specs=(in_vmem,) * 5,
        scratch_shapes=[pltpu.VMEM((features, slots), F32)],
        compiler_params=pltpu.CompilerParams(vmem_limit_bytes=40 << 20),
        cost_estimate=pl.CostEstimate(
            flops=10 * slots * features * units, bytes_accessed=9 << 20, transcendentals=slots * units
        ),
    )(
        me_c.reshape(1).astype(jnp.int32),
        own,
        other,
        held[:, 2 * width :],
        ahead_mat,
        behind_mat,
        first,
    )
    pair = pl.pallas_call(
        add_kernel,
        out_shape=jax.ShapeDtypeStruct(give.shape, BF),
        in_specs=[in_vmem] * 2,
        out_specs=in_vmem,
        compiler_params=pltpu.CompilerParams(vmem_limit_bytes=40 << 20),
    )(keep, lax.ppermute(give, "c", swap))
    plane = lax.all_to_all(pair, ("x", "y"), split_axis=0, concat_axis=0, tiled=True)
    plane, hidden, down_coef, flags, own, combine = lax.optimization_barrier(
        (plane, hidden, down_coef, flags, own, combine)
    )
    plane = jnp.sum(plane.astype(F32), axis=0)
    grad_a = dot(hidden, down_coef, 0, 0)

    feats, low_own = plane[: nz * piece].reshape(nz, piece, slots), plane[nz * piece :]
    me_z = lax.axis_index("zh")

    def block(step):
        return lax.dynamic_index_in_dim(feats, (me_z + step) % nz, 0, keepdims=False)

    def pass_on(rows, low, step):
        sent = jnp.concatenate([rows, low], axis=0).astype(BF)
        got = lax.ppermute(sent, "zh", [(i, (i + step) % nz) for i in range(nz)]).astype(F32)
        return got[:piece], got[piece:]

    far_rows, low_below = pass_on(block(2), low_own, 1)
    rows_above, low_above = pass_on(block(nz - 1), low_own, nz - 1)
    rows_below, low_far = pass_on(block(1) + far_rows, low_below, 1)
    total = block(0) + rows_above + rows_below
    low_all = low_own + low_above + low_below + low_far

    lanes = 128
    feats = total.reshape(piece, ne, CAP).transpose(1, 0, 2)
    came = lax.all_to_all(
        feats.reshape(ne, piece * CAP // lanes, lanes),
        "e",
        split_axis=0,
        concat_axis=0,
        tiled=True,
    )
    returned = came.reshape(ne, piece, CAP).transpose(1, 0, 2).reshape(piece, slots)
    input_grad = dot(combine, returned, 0, 1, lax.Precision.HIGHEST).astype(BF)

    tiled = jnp.tile(low_all, (TEN, 1))
    up_coef = (SCALE * flags * tiled.T).astype(BF)
    local = lax.dynamic_index_in_dim(
        own.reshape(ny, nx * quarter_rows, 2 * width), me_y, 0, keepdims=False
    )[:, width:]
    grad_b = dot(up_coef, local, 0, 0)
    return input_grad, grad_a[None], grad_b[None]


def solution(mesh):
    tensor, dp, expert = mesh.shape["tensor"], mesh.shape["dp"], mesh.shape["expert"]
    fine = Mesh(
        mesh.devices.reshape(dp // 4, 4, expert, tensor // 2, 2), ("zh", "x", "e", "y", "c")
    )
    units, cols = ("zh", "x", "y", "c"), ("y", "c")
    return jax.shard_map(
        on_device,
        mesh=fine,
        in_specs=(
            P("e", cols),
            P("e", cols),
            P("e", None),
            P("e", None),
            P("e"),
            P("e", None, units),
            P("e", None, units),
            P("e", units, None),
            P("e", units, None),
            P("e", None, None),
        ),
        out_specs=(P("e", units), P("e", units, None), P("e", None, cols)),
        check_vma=False,
    )
```
